256 devices in a mesh: rows: 64 (over z, y, core), tp: 4 (over x).
Axes of the slice: x: 4, y: 4, z: 8, core: 2. Of those that a mesh axis runs over, the one named last changes fastest.
Arguments:
- normed_rows: bfloat16 [16384, 8192], P('rows'), may hold values from -6 to 6
- value_weight: bfloat16 [8192, 1024], P(None, 'tp'), may hold values from -0.0625 to 0.0625
- adapter_a: bfloat16 [128, 8192, 64], P('rows', 'tp'), may hold values from -0.0625 to 0.0625
- adapter_b: bfloat16 [128, 64, 1024], P('rows', None, 'tp'), may hold values from -0.75 to 0.75
- page_table: int32 [128], replicated, may hold values from 0 to 127, as said below
- group_list: int32 [64, 64], replicated, may hold values from 0 to 127, as said below
- seg_len: int32 [64, 64], P('rows'), may hold values from 1 to 8, 256 in all within a row
- kv_len: int32 [64, 256], P('rows'), may hold values from 1 to 32, 4096 in all within a row
- queries: bfloat16 [16384, 8192], P('rows', 'tp'), may hold values from -8 to 8
- new_key: bfloat16 [16384, 1024], P('rows', 'tp'), may hold values from -8 to 8
- cache_keys: bfloat16 [16384, 32, 1024], P('rows', None, 'tp'), may hold values from -8 to 8
- cache_values: bfloat16 [16384, 32, 1024], P('rows', None, 'tp'), may hold values from -6 to 6
Outputs:
- new_value: bfloat16 [16384, 1024], P('rows', 'tp')
- attended: bfloat16 [16384, 8192], P('rows', 'tp')
The draws below stay inside these ranges and needn't reach their ends.
Inputs may be any that keep to these rules, and one draw needn't show every extreme that they name: `page_table`: each adapter has one position; the device of rows index p // 2 stores position p. `group_list`: the 64 adapters of a group are stored on 64 different indices of rows.
All inputs are finite; a program needn't handle non-finite values.
Results may differ from the reference program's by a relative error of at most 0.0048.
Values may be sent and summed in bfloat16 or wider, within the bound.
No kernel may reach another device: no remote copies, remote signals or barrier semaphores. Data moves between devices by JAX's collectives and lax.ppermute only.
A program may use at most 128 MiB of HBM per device.

```python
import math
import jax
import jax.numpy as jnp
import numpy as np
from jax import lax

D = 8192
QH = 64
KVH = 8
HEAD = 128
RANK = 64
ROWS_DEV = 256
CACHE = 32
ADP_DEV = 2
GROUPS = 64
ROWS = 16384
ADAPTERS = 128
SLOTS = 64
MOST = 8


def pick_owners(sub_key):
    return jax.random.permutation(sub_key, GROUPS)[:SLOTS]


def page_parts(key):
    order = jax.random.permutation(jax.random.fold_in(key, 21), ADAPTERS).astype(jnp.int32)
    holder = jnp.argsort(order, stable=True).astype(jnp.int32)
    sub_keys = jax.random.split(jax.random.fold_in(key, 22), GROUPS)
    owners = jax.vmap(pick_owners)(sub_keys).astype(jnp.int32)
    local = jax.random.randint(jax.random.fold_in(key, 23), (GROUPS, SLOTS), 0, ADP_DEV).astype(jnp.int32)
    listed = holder[owners * ADP_DEV + local]
    return (order, listed.astype(jnp.int32))


def draw_page_table(key, part):
    order, listed = page_parts(key)
    return order


def draw_group_list(key, part):
    order, listed = page_parts(key)
    return listed


def draw_queries(key, part):
    key = jax.random.fold_in(key, 1)
    base = jnp.clip(jax.random.normal(key, (ROWS, QH, HEAD), jnp.float32), -8.0, 8.0)
    return base.reshape(ROWS, QH * HEAD).astype(jnp.bfloat16)


def draw_cache_keys(key, part):
    key = jax.random.fold_in(key, 2)
    base = jnp.clip(jax.random.normal(key, (ROWS, CACHE, KVH, HEAD), jnp.float32), -8.0, 8.0)
    return base.reshape(ROWS, CACHE, KVH * HEAD).astype(jnp.bfloat16)


def draw_new_key(key, part):
    key = jax.random.fold_in(key, 3)
    base = jnp.clip(jax.random.normal(key, (ROWS, KVH, HEAD), jnp.float32), -8.0, 8.0)
    return base.reshape(ROWS, KVH * HEAD).astype(jnp.bfloat16)


def shard_levels(own_key, extent, cuts, low, largest):
    def one(dim, shards_of):
        draws = jax.random.uniform(jax.random.fold_in(jax.random.fold_in(own_key, 6), dim), (shards_of,), jnp.float32, low / len(cuts), largest / len(cuts))
        return jnp.repeat(jnp.exp(draws), extent[dim] // shards_of).reshape((-1,) + (1,) * (len(extent) - dim - 1))

    loudness = one(*cuts[0])
    for cut in cuts[1:]:
        loudness = loudness * one(*cut)
    return loudness


def length_profile(count, total, bound, skew):
    loads = [(1 << 20) // math.isqrt(standing ** skew) + 1 for standing in range(2, count + 1)]
    spare, given = total - bound - (count - 1), [1] * (count - 1)
    while spare > 0:
        candidates = [i for i in range(count - 1) if given[i] < bound]
        mass, left = sum([loads[i] for i in candidates]), spare
        for i in candidates:
            extra = min(bound - given[i], max(1, left * loads[i] // mass), spare)
            given[i] = given[i] + extra
            spare = spare - extra
    return np.array([bound] + given)


def ragged_sizes(own_key, count, total, reach, slope):
    if count == 2:
        one = jax.random.randint(own_key, (), max(1, total - reach), min(reach, total - 1) + 1)
        return jnp.stack([one, total - one])
    tallies = jnp.asarray(length_profile(count, total, reach, slope), jnp.int32)
    twos = (count - 1) // 2
    giver, receiver = tallies[1:1 + 2 * twos:2], tallies[2:2 + 2 * twos:2]
    slack = jnp.minimum(giver - 1, reach - receiver)
    moved = jax.random.randint(jax.random.fold_in(own_key, 1), (twos,), 0, 1 << 20) % (slack + 1)
    tallies = tallies.at[1:1 + 2 * twos:2].set(giver - moved).at[2:2 + 2 * twos:2].set(receiver + moved)
    return tallies[jax.random.permutation(jax.random.fold_in(own_key, 2), count)]


def normal_values(key, dims, deviation, reach, cuts=(), kind=jnp.bfloat16):
    entries = jax.random.normal(key, dims, jnp.float32) * deviation
    if len(cuts) > 0:
        entries = shard_levels(key, dims, cuts, -0.22, 0.18) * entries
    return jnp.clip(entries, min=-reach, max=reach).astype(kind)


def setup_inputs(seed: int = 0) -> dict:
    seeds = jax.random.split(jax.random.key(seed), 13)
    normed_rows = normal_values(seeds[0], (ROWS, D), 1.0, 6.0, ((0, 64),))
    value_weight = normal_values(seeds[1], (D, KVH * HEAD), D ** -0.5, 0.0625, ((1, 4),))
    adapter_a = normal_values(seeds[2], (ADAPTERS, D, RANK), D ** -0.5, 0.0625, ((0, 64), (1, 4)))
    adapter_b = normal_values(seeds[3], (ADAPTERS, RANK, KVH * HEAD), RANK ** -0.5, 0.75, ((0, 64), (2, 4)))
    page_table = draw_page_table(jax.random.fold_in(seeds[12], 71), 0)
    group_list = draw_group_list(jax.random.fold_in(seeds[12], 71), 0)
    seg_len = jax.vmap(lambda own: ragged_sizes(own, SLOTS, ROWS_DEV, MOST, 1))(jax.random.split(seeds[6], GROUPS)).reshape((GROUPS, SLOTS)).astype(jnp.int32)
    kv_len = jax.vmap(lambda own: ragged_sizes(own, ROWS_DEV, ROWS_DEV * CACHE // 2, CACHE, 2))(jax.random.split(seeds[7], GROUPS)).reshape((GROUPS, ROWS_DEV)).astype(jnp.int32)
    queries = draw_queries(jax.random.fold_in(seeds[12], 71), 0)
    new_key = draw_new_key(jax.random.fold_in(seeds[12], 71), 0)
    cache_keys = draw_cache_keys(jax.random.fold_in(seeds[12], 71), 0)
    cache_values = normal_values(seeds[11], (ROWS, CACHE, KVH * HEAD), 1.0, 6.0, ((0, 64), (2, 4)))
    return {"normed_rows": normed_rows, "value_weight": value_weight, "adapter_a": adapter_a, "adapter_b": adapter_b, "page_table": page_table, "group_list": group_list, "seg_len": seg_len, "kv_len": kv_len, "queries": queries, "new_key": new_key, "cache_keys": cache_keys, "cache_values": cache_values}


def segment_rows(lens, rows_count):
    ends = jnp.cumsum(lens).astype(jnp.int32)
    rowpos = jnp.arange(rows_count, dtype=jnp.int32)
    return lax.optimization_barrier(jnp.sum((rowpos[:, None] >= ends[None, :]).astype(jnp.int32), axis=1)).astype(jnp.int32)

def attend(query_rows, key_new, keys, values, value_new, lengths):
    count = query_rows.shape[0]
    heads_kv = key_new.shape[1] // HEAD
    group = query_rows.shape[1] // key_new.shape[1]
    scale = 1.0 / math.sqrt(HEAD)
    q_four = query_rows.reshape(count, heads_kv, group, HEAD).astype(jnp.float32)
    k_four = keys.reshape(count, -1, heads_kv, HEAD).astype(jnp.float32)
    v_four = values.reshape(count, -1, heads_kv, HEAD).astype(jnp.float32)
    k_own = key_new.reshape(count, heads_kv, HEAD).astype(jnp.float32)
    v_own = value_new.reshape(count, heads_kv, HEAD).astype(jnp.float32)
    score = jnp.einsum('rhgd,rchd->rhgc', q_four, k_four) * scale
    own = jnp.einsum('rhgd,rhd->rhg', q_four, k_own) * scale
    valid = (jnp.arange(keys.shape[1], dtype=jnp.int32)[None, :] < lengths[:, None])[:, None, None, :]
    top = jnp.maximum(lax.optimization_barrier(jnp.max(jnp.where(valid, score, -jnp.inf), axis=-1)), own)
    expd = jnp.where(valid, jnp.exp(score - top[..., None]), 0.0)
    exp_own = jnp.exp(own - top)
    total = lax.optimization_barrier(jnp.sum(expd, axis=-1)) + exp_own
    weight = lax.optimization_barrier(expd.astype(jnp.bfloat16)).astype(jnp.float32)
    weight_own = lax.optimization_barrier(exp_own.astype(jnp.bfloat16)).astype(jnp.float32)
    context = jnp.einsum('rhgc,rchd->rhgd', weight, v_four) + weight_own[..., None] * v_own[:, :, None, :]
    return (context / total[..., None]).astype(jnp.bfloat16).reshape(count, -1)

def reference(normed_rows, value_weight, adapter_a, adapter_b, page_table, group_list, seg_len, kv_len, queries, new_key, cache_keys, cache_values):
    width_kv = KVH * HEAD

    def one_group(items):
        rows_x, rows_q, rows_k, rows_ck, rows_cv, lens_kv, lens_seg, listed = items
        segment = segment_rows(lens_seg, ROWS_DEV)
        stored = page_table[listed[segment]]
        a_rows = adapter_a[stored].astype(jnp.float32)
        low = jnp.einsum('rd,rdk->rk', rows_x.astype(jnp.float32), a_rows)
        low = lax.optimization_barrier(low.astype(jnp.bfloat16)).astype(jnp.float32)
        b_rows = adapter_b[stored].astype(jnp.float32)
        delta = jnp.einsum('rk,rkv->rv', low, b_rows)
        delta = lax.optimization_barrier(delta.astype(jnp.bfloat16)).astype(jnp.float32)
        base = jnp.dot(rows_x, value_weight, preferred_element_type=jnp.float32)
        value_new = (base + delta).astype(jnp.bfloat16)
        result = attend(rows_q, rows_k, rows_ck, rows_cv, value_new, lens_kv)
        return (value_new, result)
    stacked = (normed_rows.reshape(GROUPS, ROWS_DEV, D), queries.reshape(GROUPS, ROWS_DEV, QH * HEAD), new_key.reshape(GROUPS, ROWS_DEV, width_kv), cache_keys.reshape(GROUPS, ROWS_DEV, CACHE, width_kv), cache_values.reshape(GROUPS, ROWS_DEV, CACHE, width_kv), kv_len, seg_len, group_list)
    new_value, attended = lax.map(one_group, stacked)
    return (new_value.reshape(ROWS, width_kv), attended.reshape(ROWS, QH * HEAD))
```

```python
import functools
import math

import jax
import jax.numpy as jnp
from jax import lax
from jax.experimental import pallas as pl
from jax.experimental.pallas import tpu as pltpu
from jax.sharding import PartitionSpec as P

HEAD = 128
MOST = 8
f32 = jnp.float32
bf16 = jnp.bfloat16
i32 = jnp.int32
NT = (((1,), (1,)), ((), ()))
VMEM_LIMIT = 48 * 1024 * 1024


def params():
    return pltpu.CompilerParams(vmem_limit_bytes=VMEM_LIMIT)


def iota(shape, dim):
    return lax.broadcasted_iota(i32, shape, dim)


def segment_rows(group, glist_ref, table_ref, lens_ref):
    slots = lens_ref.shape[1]
    adapters = table_ref.shape[1]
    listed = glist_ref[pl.ds(group, 1), :]
    hit = (iota((adapters, slots), 0) == listed).astype(f32)
    table = jnp.broadcast_to(table_ref[...].astype(f32), (8, adapters))
    position = jnp.dot(table, hit, preferred_element_type=f32)[:1]
    owner = jnp.right_shift(position.astype(i32), 1).astype(f32)
    lens = lens_ref[...].astype(f32)
    before = (iota((slots, slots), 0) < iota((slots, slots), 1)).astype(f32)
    start = jnp.dot(jnp.broadcast_to(lens, (8, slots)), before, preferred_element_type=f32)[:1]
    return owner, start, lens


def place_kernel(where_ref, glist_ref, table_ref, lens_ref, x_ref, out_ref, placing):
    slots = lens_ref.shape[1]
    rows = x_ref.shape[0]
    count = out_ref.shape[0]

    @pl.when(pl.program_id(0) == 0)
    def _():
        owner, start, lens = segment_rows(where_ref[0], glist_ref, table_ref, lens_ref)
        slot = iota((count, 1), 0)
        mine = owner == jnp.right_shift(slot, 3).astype(f32)
        first = jnp.sum(jnp.where(mine, start, 0.0), axis=1, keepdims=True)
        length = jnp.sum(jnp.where(mine, lens, 0.0), axis=1, keepdims=True)
        within = jnp.bitwise_and(slot, MOST - 1).astype(f32)
        source = jnp.where(within < length, first + within, -1.0)
        placing[...] = (iota((count, rows), 1).astype(f32) == source).astype(bf16)

    out_ref[...] = jnp.dot(placing[...], x_ref[...], preferred_element_type=f32).astype(bf16)


def place(where, glist, table, lens, rows_x, part, count):
    rows = rows_x.shape[0]
    steps = 4
    wide = part // steps
    return pl.pallas_call(
        place_kernel,
        out_shape=jax.ShapeDtypeStruct((count, part), bf16),
        grid_spec=pltpu.PrefetchScalarGridSpec(
            num_scalar_prefetch=1,
            grid=(steps,),
            in_specs=[
                pl.BlockSpec(glist.shape, lambda i, s: (0, 0)),
                pl.BlockSpec(table.shape, lambda i, s: (0, 0)),
                pl.BlockSpec(lens.shape, lambda i, s: (0, 0)),
                pl.BlockSpec((rows, wide), lambda i, s: (0, s[1] * steps + i)),
            ],
            out_specs=pl.BlockSpec((count, wide), lambda i, s: (0, i)),
            scratch_shapes=[pltpu.VMEM((count, rows), bf16)],
        ),
        compiler_params=params(),
    )(where, glist, table, lens, rows_x)


def unplace_kernel(where_ref, glist_ref, table_ref, lens_ref, out_ref):
    rows, count = out_ref.shape
    owner, start, lens = segment_rows(where_ref[0], glist_ref, table_ref, lens_ref)
    row = iota((rows, 1), 0).astype(f32)
    inside = (row >= start) & (row < start + lens)
    target = jnp.sum(jnp.where(inside, owner * MOST + row - start, 0.0), axis=1, keepdims=True)
    out_ref[...] = (iota((rows, count), 1).astype(f32) == target).astype(bf16)


def unplace(where, glist, table, lens, rows, count):
    return pl.pallas_call(
        unplace_kernel,
        out_shape=jax.ShapeDtypeStruct((rows, count), bf16),
        in_specs=[pl.BlockSpec(memory_space=pltpu.SMEM)]
        + [pl.BlockSpec(memory_space=pltpu.VMEM)] * 3,
        out_specs=pl.BlockSpec(memory_space=pltpu.VMEM),
        compiler_params=params(),
    )(where, glist, table, lens)


def second_of_slots(owner, glist_ref, table_ref, count):
    groups, adapters = glist_ref.shape[0], table_ref.shape[1]
    ids = iota((1, adapters), 1)
    second = jnp.max(jnp.where(table_ref[...] == 2 * owner + 1, ids, -1), axis=1, keepdims=True)
    uses = (glist_ref[...] == second).astype(f32)
    uses = jnp.max(uses, axis=1, keepdims=True)
    spread = (jnp.right_shift(iota((count, groups), 0), 3) == iota((count, groups), 1)).astype(f32)
    wide = jnp.dot(spread, jnp.broadcast_to(uses, (groups, 128)), preferred_element_type=f32)
    return wide > 0.5


def low_kernel(where_ref, glist_ref, table_ref, x_ref, a_ref, out_ref):
    count, half = x_ref.shape[0], x_ref.shape[0] // 2
    rank = a_ref.shape[0] // 2
    second = second_of_slots(where_ref[0], glist_ref, table_ref, count)
    each = lax.dot_general(x_ref[...], a_ref[...], NT, preferred_element_type=f32)
    turned = pltpu.roll(each, rank, 1)
    left = jnp.where(second, turned, each)
    right = jnp.where(second, each, turned)
    out_ref[...] = jnp.where(iota((half, 2 * rank), 1) < rank, left[:half], right[half:])


def delta_kernel(where_ref, glist_ref, table_ref, p0, p1, p2, p3, b_ref, out_ref):
    count = out_ref.shape[0]
    half, rank = count // 2, b_ref.shape[0] // 2
    second = second_of_slots(where_ref[0], glist_ref, table_ref, count)
    low = (p0[...] + p1[...]) + (p2[...] + p3[...])
    turned = pltpu.roll(low, rank, 1)
    lane = iota((half, 2 * rank), 1) < rank
    both = jnp.concatenate([jnp.where(lane, low, turned), jnp.where(lane, turned, low)], axis=0)
    keep = (iota((count, 2 * rank), 1) >= rank) == second
    low = jnp.where(keep, both, 0.0).astype(bf16)
    out_ref[...] = jnp.dot(low, b_ref[...], preferred_element_type=f32).astype(bf16)


def whole_call(kernel, shape, dtype, *args):
    return pl.pallas_call(
        kernel,
        out_shape=jax.ShapeDtypeStruct(shape, dtype),
        in_specs=[pl.BlockSpec(memory_space=pltpu.SMEM)]
        + [pl.BlockSpec(memory_space=pltpu.VMEM)] * (len(args) - 1),
        out_specs=pl.BlockSpec(memory_space=pltpu.VMEM),
        compiler_params=params(),
    )(*args)


def attend_kernel(scale, q_ref, nk_ref, k_ref, v_ref, len_ref, ctx_ref, own_ref):
    rows, cache, width = k_ref.shape
    kv_heads = width // HEAD
    group = q_ref.shape[1] // width
    many = 8 * group
    row = jnp.bitwise_and(iota((many, 128), 0), 7)
    lane = iota((many, 128), 1)
    upper = row >= 4
    place_ok = jnp.right_shift(lane, 5) == jnp.bitwise_and(row, 3)
    cell = jnp.bitwise_and(lane, cache - 1)
    lane8 = iota((8, 128), 1)
    for pair in range(rows // 16):
        q16 = q_ref[pl.ds(pair * 16, 16), :].astype(f32)
        nk16 = nk_ref[pl.ds(pair * 16, 16), :].astype(f32)
        for sub in range(2):
            base = pair * 16 + sub * 8
            q8 = q16[sub * 8 : sub * 8 + 8]
            nk8 = nk16[sub * 8 : sub * 8 + 8]
            keys = k_ref[pl.ds(base, 8)].reshape(8 * cache, width)
            values = v_ref[pl.ds(base, 8)].reshape(8 * cache, width)
            lens = jnp.concatenate([len_ref[pl.ds(base, 8), :]] * group, axis=0)
            valid = place_ok & (cell < lens)
            own_tile = jnp.zeros((8, 128), f32)
            for h in range(kv_heads):
                cut = slice(h * HEAD, (h + 1) * HEAD)
                q = jnp.concatenate(
                    [q8[:, (h * group + g) * HEAD : (h * group + g + 1) * HEAD] for g in range(group)],
                    axis=0,
                )
                score = lax.dot_general(
                    q.astype(bf16), keys[:, cut], NT, preferred_element_type=f32
                )
                score = jnp.where(upper, score[:, 128:], score[:, :128]) * scale
                score = jnp.where(valid, score, -1e30)
                own = jnp.sum(
                    q * jnp.concatenate([nk8[:, cut]] * group, axis=0), axis=1, keepdims=True
                ) * scale
                top = jnp.maximum(jnp.max(score, axis=1, keepdims=True), own)
                weight = jnp.where(valid, jnp.exp(score - top), 0.0)
                e_own = jnp.exp(own - top)
                inv = 1.0 / (jnp.sum(weight, axis=1, keepdims=True) + e_own)
                split = jnp.concatenate(
                    [jnp.where(upper, 0.0, weight), jnp.where(upper, weight, 0.0)], axis=1
                ).astype(bf16)
                ctx = jnp.dot(split, values[:, cut], preferred_element_type=f32) * inv
                w_own = e_own.astype(bf16).astype(f32) * inv
                for g in range(group):
                    head = h * group + g
                    ctx_ref[pl.ds(base, 8), head * HEAD : (head + 1) * HEAD] = ctx[g * 8 : g * 8 + 8]
                    own_tile = jnp.where(lane8 == head, w_own[g * 8 : g * 8 + 8], own_tile)
            own_ref[pl.ds(base, 8), :] = own_tile


def attend(queries, new_key, cache_keys, cache_values, lengths):
    rows, wide = queries.shape
    cache, width = cache_keys.shape[1:]
    step = 32
    return pl.pallas_call(
        functools.partial(attend_kernel, 1.0 / math.sqrt(HEAD)),
        out_shape=(
            jax.ShapeDtypeStruct((rows, wide), f32),
            jax.ShapeDtypeStruct((rows, 128), f32),
        ),
        grid=(rows // step,),
        in_specs=[
            pl.BlockSpec((step, wide), lambda i: (i, 0)),
            pl.BlockSpec((step, width), lambda i: (i, 0)),
            pl.BlockSpec((step, cache, width), lambda i: (i, 0, 0)),
            pl.BlockSpec((step, cache, width), lambda i: (i, 0, 0)),
            pl.BlockSpec((step, 1), lambda i: (i, 0)),
        ],
        out_specs=(
            pl.BlockSpec((step, wide), lambda i: (i, 0)),
            pl.BlockSpec((step, 128), lambda i: (i, 0)),
        ),
        compiler_params=params(),
    )(queries, new_key, cache_keys, cache_values, lengths)


def finish_kernel(un_ref, delta_ref, base_ref, ctx_ref, own_ref, value_ref, out_ref):
    heads = out_ref.shape[1] // HEAD
    group = out_ref.shape[1] // value_ref.shape[1]
    delta = jnp.dot(un_ref[...], delta_ref[...], preferred_element_type=f32)
    value = (base_ref[...] + delta).astype(bf16)
    value_ref[...] = value
    value = value.astype(f32)
    for head in range(heads):
        kv = head // group
        cut = slice(head * HEAD, (head + 1) * HEAD)
        out_ref[:, cut] = (
            ctx_ref[:, cut] + own_ref[:, head : head + 1] * value[:, kv * HEAD : (kv + 1) * HEAD]
        ).astype(bf16)


def finish(un, delta, base, ctx, own):
    rows, wide = ctx.shape
    step = 64
    by_row = lambda n: pl.BlockSpec((step, n), lambda i: (i, 0))
    return pl.pallas_call(
        finish_kernel,
        out_shape=(
            jax.ShapeDtypeStruct(base.shape, bf16),
            jax.ShapeDtypeStruct((rows, wide), bf16),
        ),
        grid=(rows // step,),
        in_specs=[
            by_row(un.shape[1]),
            pl.BlockSpec(delta.shape, lambda i: (0, 0)),
            by_row(base.shape[1]),
            by_row(wide),
            by_row(128),
        ],
        out_specs=(by_row(base.shape[1]), by_row(wide)),
        compiler_params=params(),
    )(un, delta, base, ctx, own)


def body(
    normed_rows,
    value_weight,
    adapter_a,
    adapter_b,
    page_table,
    group_list,
    seg_len,
    kv_len,
    queries,
    new_key,
    cache_keys,
    cache_values,
):
    tp = lax.axis_size("tp")
    groups = lax.axis_size("rows")
    rows = normed_rows.shape[0]
    part = normed_rows.shape[1] // tp
    per_owner, _, rank = adapter_a.shape
    width = adapter_b.shape[2]
    count = groups * MOST
    where = jnp.stack([lax.axis_index("rows"), lax.axis_index("tp")]).astype(i32)
    table = page_table.reshape(1, -1)
    a_turned = jnp.swapaxes(adapter_a, 1, 2).reshape(per_owner * rank, part)
    b_flat = adapter_b.reshape(per_owner * rank, width)

    placed = place(where, group_list, table, seg_len, normed_rows, part, count)
    arrived = lax.all_to_all(
        placed.reshape(groups, MOST, part), "rows", split_axis=0, concat_axis=0, tiled=True
    ).reshape(count, part)

    un = unplace(where, group_list, table, seg_len, rows, count)
    base = jnp.dot(normed_rows, value_weight, preferred_element_type=f32)
    ctx, own = attend(queries, new_key, cache_keys, cache_values, kv_len.reshape(-1, 1))

    arrived, un, base, ctx, own = lax.optimization_barrier((arrived, un, base, ctx, own))
    partial = whole_call(
        low_kernel, (count // 2, 2 * rank), f32, where, group_list, table, arrived, a_turned
    )
    others = [
        lax.ppermute(partial, "tp", [(j, (j + k) % tp) for j in range(tp)]) for k in range(1, tp)
    ]
    delta_out = whole_call(
        delta_kernel, (count, width), bf16, where, group_list, table, partial, *others, b_flat
    )
    delta = lax.all_to_all(
        delta_out.reshape(groups, MOST, width), "rows", split_axis=0, concat_axis=0, tiled=True
    ).reshape(count, width)
    return finish(un, delta, base, ctx, own)


def solution(mesh):
    return jax.shard_map(
        body,
        mesh=mesh,
        in_specs=(
            P("rows", None),
            P(None, "tp"),
            P("rows", "tp", None),
            P("rows", None, "tp"),
            P(),
            P(),
            P("rows", None),
            P("rows", None),
            P("rows", "tp"),
            P("rows", "tp"),
            P("rows", None, "tp"),
            P("rows", None, "tp"),
        ),
        out_specs=(P("rows", "tp"), P("rows", "tp")),
        check_vma=False,
    )
```

```python
import functools
import math

import jax
import jax.numpy as jnp
from jax import lax
from jax.experimental import pallas as pl
from jax.experimental.pallas import tpu as pltpu
from jax.sharding import PartitionSpec as P

HEAD = 128
PLANE = 8
MOST = 8
f32 = jnp.float32
bf16 = jnp.bfloat16
i32 = jnp.int32
NT = (((1,), (1,)), ((), ()))
MIB = 1024 * 1024


FREE = pl.CostEstimate(flops=0, bytes_accessed=0, transcendentals=0)


def params(mib=12):
    return pltpu.CompilerParams(vmem_limit_bytes=mib * MIB)


def iota(shape, dim):
    return lax.broadcasted_iota(i32, shape, dim)


def segment_rows(meta):
    slots, groups = meta.slots, meta.groups
    adapters = meta.adapters
    listed = meta.ref[pl.ds(lax.axis_index("rows"), 1), :slots]
    hit = (iota((adapters, slots), 0) == listed).astype(f32)
    table = jnp.broadcast_to(meta.table().astype(f32), (8, adapters))
    position = jnp.dot(table, hit, preferred_element_type=f32)[:1]
    owner = jnp.right_shift(position.astype(i32), 1).astype(f32)
    lens = meta.ref[groups + 1 : groups + 2, :slots].astype(f32)
    before = (iota((slots, slots), 0) < iota((slots, slots), 1)).astype(f32)
    start = jnp.dot(jnp.broadcast_to(lens, (8, slots)), before, preferred_element_type=f32)[:1]
    return owner, start, lens


class Meta:
    def __init__(self, ref, groups, slots, adapters):
        self.ref, self.groups, self.slots, self.adapters = ref, groups, slots, adapters

    def table(self):
        return self.ref[self.groups : self.groups + 1, : self.adapters]


def column(plane):
    rows = lax.axis_index("rows")
    at = lax.rem(rows, plane)
    return lax.div(rows, plane), lax.div(at, 2), lax.rem(at, 2)


def owner_at(z, k, y, core, plane):
    half = plane // 2
    owner_y = lax.rem(lax.rem(k, half) + y, half)
    owner_core = lax.rem(lax.div(k, half) + core, 2)
    return z * plane + owner_y * 2 + owner_core


def slot_owner(slot, y, core, plane):
    k = lax.rem(jnp.right_shift(slot, 3), plane)
    return owner_at(lax.div(slot, plane * MOST), k, y, core, plane)


def place_kernel(plane, sizes, meta_ref, x_ref, out_ref, token_ref):
    count = out_ref.shape[0]
    rows = x_ref.shape[0]
    token_ref[...] = jnp.zeros_like(token_ref)
    owner, start, lengths = segment_rows(Meta(meta_ref, *sizes))
    _, y, core = column(plane)
    slot = iota((count, 1), 0)
    mine = owner == slot_owner(slot, y, core, plane).astype(f32)
    begin = jnp.sum(jnp.where(mine, start, 0.0), axis=1, keepdims=True)
    length = jnp.sum(jnp.where(mine, lengths, 0.0), axis=1, keepdims=True)
    within = jnp.bitwise_and(slot, MOST - 1).astype(f32)
    source = jnp.where(within < length, begin + within, -1.0)
    placing = (iota((count, rows), 1).astype(f32) == source).astype(bf16)
    out_ref[...] = jnp.dot(placing, x_ref[...], preferred_element_type=f32).astype(bf16)


def place(sizes, meta, x_part, count):
    part = x_part.shape[1]
    vmem = pl.BlockSpec(memory_space=pltpu.VMEM)
    return pl.pallas_call(
        functools.partial(place_kernel, PLANE, sizes),
        out_shape=(
            jax.ShapeDtypeStruct((count, part), bf16),
            jax.ShapeDtypeStruct((8, 128), i32),
        ),
        in_specs=[vmem, vmem],
        out_specs=(vmem, vmem),
        compiler_params=params(),
    )(meta, x_part)


def unplace_kernel(plane, sizes, meta_ref, token_ref, out_ref):
    rows, count = out_ref.shape
    owner, start, lens = segment_rows(Meta(meta_ref, *sizes))
    _, y, core = column(plane)
    row = iota((rows, 1), 0).astype(f32)
    inside = (row >= start) & (row < start + lens)
    target = jnp.sum(jnp.where(inside, owner * MOST + row - start, 0.0), axis=1, keepdims=True)
    slot = iota((1, count), 1)
    meant = slot_owner(slot, y, core, plane) * MOST + jnp.bitwise_and(slot, MOST - 1)
    out_ref[...] = (meant.astype(f32) == target).astype(bf16)


def choose_kernel(plane, sizes, meta_ref, token_ref, out_ref):
    meta = Meta(meta_ref, *sizes)
    count = out_ref.shape[0]
    planes = meta.groups // plane
    z, y, core = column(plane)
    at = lax.rem(lax.axis_index("rows"), plane)
    listed = jnp.concatenate(
        [meta_ref[pl.ds(p * plane + at, 1), : meta.slots] for p in range(planes)], axis=0
    )
    table = meta.table()
    ids = iota((1, meta.adapters), 1)
    lane = iota((planes, 128), 1)
    uses = jnp.zeros((planes, 128), f32)
    for k in range(plane):
        owner = owner_at(z, k, y, core, plane)
        second = jnp.max(jnp.where(table == 2 * owner + 1, ids, -1), axis=1, keepdims=True)
        hit = jnp.max((listed == second).astype(f32), axis=1, keepdims=True)
        uses = jnp.where(lane == k, hit, uses)
    row = iota((count, 1), 0)
    both = 2 * MOST
    k_of = lax.div(row, both * planes) * 2 + jnp.bitwise_and(jnp.right_shift(row, 3), 1)
    from_z = lax.rem(lax.div(row, both), planes)
    spread = (from_z == iota((count, planes), 1)).astype(f32)
    wide = jnp.dot(spread, uses, preferred_element_type=f32)
    mine = iota((count, 128), 1) == k_of
    out_ref[...] = jnp.broadcast_to(
        jnp.sum(jnp.where(mine, wide, 0.0), axis=1, keepdims=True), out_ref.shape
    )


def low_kernel(plane, choice_ref, x_ref, near_ref, far_ref, out_ref):
    count, part = x_ref.shape
    half, both = out_ref.shape
    rank = both // 2
    tile = 2 * MOST
    stride = plane * MOST
    pairs = []
    for pair in range(plane // 2):
        ref = near_ref if pair < plane // 4 else far_ref
        first = pair % (plane // 4) * 2
        a = jnp.concatenate([ref[first, :part], ref[first + 1, :part]], axis=1)
        x = jnp.concatenate(
            [x_ref[at : at + tile, :] for at in range(pair * tile, count, stride)], axis=0
        )
        each = jnp.dot(x, a, preferred_element_type=f32)
        odd = jnp.bitwise_and(iota((each.shape[0], both), 0), MOST) > 0
        pairs.append(jnp.where(odd, each[:, both:], each[:, :both]))
    total = jnp.concatenate(pairs, axis=0)
    second = choice_ref[...] > 0.5
    turned = pltpu.roll(total, rank, 1)
    left = jnp.where(second, turned, total)
    right = jnp.where(second, total, turned)
    out_ref[...] = jnp.where(iota((half, both), 1) < rank, left[:half], right[half:])


def delta_kernel(plane, choice_ref, p0, p1, p2, p3, maps_ref, out_ref):
    count, width = out_ref.shape
    half, both = p0.shape
    rank = both // 2
    tile = 2 * MOST
    stride = plane * MOST
    low = (p0[...] + p1[...]) + (p2[...] + p3[...])
    turned = pltpu.roll(low, rank, 1)
    lane = iota((half, both), 1) < rank
    twice = jnp.concatenate([jnp.where(lane, low, turned), jnp.where(lane, turned, low)], axis=0)
    keep = (iota((count, both), 1) >= rank) == (choice_ref[...] > 0.5)
    low = jnp.where(keep, twice, 0.0)
    odd = jnp.bitwise_and(iota((count, both), 0), MOST) > 0
    spread = jnp.concatenate(
        [jnp.where(odd, 0.0, low), jnp.where(odd, low, 0.0)], axis=1
    ).astype(bf16)
    many = count // (plane // 2)
    for pair in range(plane // 2):
        wide = [
            jnp.concatenate([maps_ref[k, at : at + both] for at in range(0, width, both)], axis=1)
            for k in (2 * pair, 2 * pair + 1)
        ]
        got = jnp.dot(
            spread[pair * many : (pair + 1) * many],
            jnp.concatenate(wide, axis=0),
            preferred_element_type=f32,
        ).astype(bf16)
        for i in range(many // tile):
            at = i * stride + pair * tile
            out_ref[at : at + tile, :] = got[i * tile : (i + 1) * tile]


def vmem_call(kernel, shape, dtype, *args):
    return pl.pallas_call(
        kernel,
        out_shape=jax.ShapeDtypeStruct(shape, dtype),
        in_specs=[pl.BlockSpec(memory_space=pltpu.VMEM)] * len(args),
        out_specs=pl.BlockSpec(memory_space=pltpu.VMEM),
        cost_estimate=FREE,
        compiler_params=params(),
    )(*args)


def attend_kernel(scale, q_ref, nk_ref, k_ref, v_ref, len_ref, ctx_ref, own_ref):
    rows, cache, width = k_ref.shape
    kv_heads = width // HEAD
    group = q_ref.shape[1] // width
    many = 8 * group
    row = jnp.bitwise_and(iota((many, 128), 0), 7)
    lane = iota((many, 128), 1)
    upper = row >= 4
    place_ok = jnp.right_shift(lane, 5) == jnp.bitwise_and(row, 3)
    cell = jnp.bitwise_and(lane, cache - 1)
    lane8 = iota((8, 128), 1)
    for pair in range(rows // 16):
        q16 = q_ref[pl.ds(pair * 16, 16), :].astype(f32)
        nk16 = nk_ref[pl.ds(pair * 16, 16), :].astype(f32)
        for sub in range(2):
            base = pair * 16 + sub * 8
            q8 = q16[sub * 8 : sub * 8 + 8]
            nk8 = nk16[sub * 8 : sub * 8 + 8]
            keys = k_ref[pl.ds(base, 8)].reshape(8 * cache, width)
            values = v_ref[pl.ds(base, 8)].reshape(8 * cache, width)
            lens = jnp.concatenate([len_ref[pl.ds(base, 8), :]] * group, axis=0)
            valid = place_ok & (cell < lens)
            own_tile = jnp.zeros((8, 128), f32)
            for h in range(kv_heads):
                cut = slice(h * HEAD, (h + 1) * HEAD)
                q = jnp.concatenate(
                    [q8[:, (h * group + g) * HEAD : (h * group + g + 1) * HEAD] for g in range(group)],
                    axis=0,
                )
                score = lax.dot_general(
                    q.astype(bf16), keys[:, cut], NT, preferred_element_type=f32
                )
                score = jnp.where(upper, score[:, 128:], score[:, :128]) * scale
                score = jnp.where(valid, score, -1e30)
                own = jnp.sum(
                    q * jnp.concatenate([nk8[:, cut]] * group, axis=0), axis=1, keepdims=True
                ) * scale
                top = jnp.maximum(jnp.max(score, axis=1, keepdims=True), own)
                weight = jnp.where(valid, jnp.exp(score - top), 0.0)
                e_own = jnp.exp(own - top)
                inv = 1.0 / (jnp.sum(weight, axis=1, keepdims=True) + e_own)
                split = jnp.concatenate(
                    [jnp.where(upper, 0.0, weight), jnp.where(upper, weight, 0.0)], axis=1
                ).astype(bf16)
                ctx = jnp.dot(split, values[:, cut], preferred_element_type=f32) * inv
                w_own = e_own.astype(bf16).astype(f32) * inv
                for g in range(group):
                    head = h * group + g
                    ctx_ref[pl.ds(base, 8), head * HEAD : (head + 1) * HEAD] = ctx[g * 8 : g * 8 + 8]
                    own_tile = jnp.where(lane8 == head, w_own[g * 8 : g * 8 + 8], own_tile)
            own_ref[pl.ds(base, 8), :] = own_tile


def attend(queries, new_key, cache_keys, cache_values, lengths):
    rows, wide = queries.shape
    cache, width = cache_keys.shape[1:]
    step = 32
    return pl.pallas_call(
        functools.partial(attend_kernel, 1.0 / math.sqrt(HEAD)),
        out_shape=(
            jax.ShapeDtypeStruct((rows, wide), f32),
            jax.ShapeDtypeStruct((rows, 128), f32),
        ),
        grid=(rows // step,),
        in_specs=[
            pl.BlockSpec((step, wide), lambda i: (i, 0)),
            pl.BlockSpec((step, width), lambda i: (i, 0)),
            pl.BlockSpec((step, cache, width), lambda i: (i, 0, 0)),
            pl.BlockSpec((step, cache, width), lambda i: (i, 0, 0)),
            pl.BlockSpec((step, 1), lambda i: (i, 0)),
        ],
        out_specs=(
            pl.BlockSpec((step, wide), lambda i: (i, 0)),
            pl.BlockSpec((step, 128), lambda i: (i, 0)),
        ),
        cost_estimate=FREE,
        compiler_params=params(),
    )(queries, new_key, cache_keys, cache_values, lengths)


def finish_kernel(un_ref, delta_ref, base_ref, ctx_ref, own_ref, value_ref, out_ref):
    heads = out_ref.shape[1] // HEAD
    group = out_ref.shape[1] // value_ref.shape[1]
    delta = jnp.dot(un_ref[...], delta_ref[...], preferred_element_type=f32)
    value = (base_ref[...] + delta).astype(bf16)
    value_ref[...] = value
    value = value.astype(f32)
    for head in range(heads):
        kv = head // group
        cut = slice(head * HEAD, (head + 1) * HEAD)
        out_ref[:, cut] = (
            ctx_ref[:, cut] + own_ref[:, head : head + 1] * value[:, kv * HEAD : (kv + 1) * HEAD]
        ).astype(bf16)


def finish(un, delta, base, ctx, own):
    rows, wide = ctx.shape
    step = 64
    by_row = lambda n: pl.BlockSpec((step, n), lambda i: (i, 0))
    whole = lambda a: pl.BlockSpec(a.shape, lambda i: (0, 0))
    return pl.pallas_call(
        finish_kernel,
        out_shape=(
            jax.ShapeDtypeStruct(base.shape, bf16),
            jax.ShapeDtypeStruct((rows, wide), bf16),
        ),
        grid=(rows // step,),
        in_specs=[
            by_row(un.shape[1]),
            whole(delta),
            by_row(base.shape[1]),
            by_row(wide),
            by_row(128),
        ],
        out_specs=(by_row(base.shape[1]), by_row(wide)),
        compiler_params=params(),
    )(un, delta, base, ctx, own)


def body(
    normed_rows,
    value_weight,
    adapter_a,
    adapter_b,
    page_table,
    group_list,
    seg_len,
    kv_len,
    queries,
    new_key,
    cache_keys,
    cache_values,
):
    tp = lax.axis_size("tp")
    groups = lax.axis_size("rows")
    planes = groups // PLANE
    rows = normed_rows.shape[0]
    part = normed_rows.shape[1] // tp
    per_owner, _, rank = adapter_a.shape
    width = adapter_b.shape[2]
    count = groups * MOST
    slots, adapters = group_list.shape[1], page_table.shape[0]
    sizes = (groups, slots, adapters)
    wide = lambda x: jnp.pad(x, ((0, 0), (0, 128 - x.shape[1])))
    meta = jnp.concatenate([wide(group_list), wide(page_table.reshape(1, -1)), wide(seg_len)], axis=0)
    columns = [[z * PLANE + at for z in range(planes)] for at in range(PLANE)]
    ring = PLANE // 2

    def shift_y(x, dy):
        pairs = []
        for r in range(groups):
            z, y, c = r // PLANE, r % PLANE // 2, r % 2
            pairs.append((z * PLANE + (y + dy) % ring * 2 + c, r))
        return lax.ppermute(x, "rows", pairs)

    def over_z(x):
        wide = x.shape[1]
        x = lax.all_to_all(
            x.reshape(planes, count // planes, wide),
            "rows",
            split_axis=0,
            concat_axis=0,
            axis_index_groups=columns,
            tiled=True,
        )
        return x.reshape(count, wide)

    x_part = lax.dynamic_slice_in_dim(normed_rows, lax.axis_index("tp") * part, part, 1)
    placed, token = place(sizes, meta, x_part, count)
    arrived = over_z(placed)

    token, meta, adapter_a, adapter_b, normed_rows = lax.optimization_barrier(
        (token, meta, adapter_a, adapter_b, normed_rows)
    )
    both = per_owner * rank
    choice = vmem_call(
        functools.partial(choose_kernel, PLANE, sizes), (count, both), f32, meta, token
    )
    un = vmem_call(functools.partial(unplace_kernel, PLANE, sizes), (rows, count), bf16, meta, token)
    packed = jnp.concatenate(
        [jnp.swapaxes(adapter_a, 0, 1).reshape(part, both)]
        + [adapter_b.reshape(both, width)[:, at : at + both] for at in range(0, width, both)],
        axis=0,
    )
    near = [packed] + [shift_y(packed, dy) for dy in range(1, ring)]
    packed, un, choice, queries = lax.optimization_barrier((packed, un, choice, queries))
    ctx, own = attend(queries, new_key, cache_keys, cache_values, kv_len.reshape(-1, 1))
    *near, ctx, own = lax.optimization_barrier((*near, ctx, own))
    near = jnp.stack(near)
    far = lax.ppermute(near, "rows", [(r ^ 1, r) for r in range(groups)])
    base = jnp.dot(normed_rows, value_weight, preferred_element_type=f32)
    b_maps = jnp.concatenate([near[:, part:], far[:, part:]], axis=0)
    arrived, un, base, ctx, own, choice, near, far, b_maps = lax.optimization_barrier(
        (arrived, un, base, ctx, own, choice, near, far, b_maps)
    )

    partial = vmem_call(
        functools.partial(low_kernel, PLANE), (count // 2, both), f32, choice, arrived, near, far
    )
    others = [
        lax.ppermute(partial, "tp", [(j, (j + k) % tp) for j in range(tp)]) for k in range(1, tp)
    ]
    out = vmem_call(
        functools.partial(delta_kernel, PLANE),
        (count, width),
        bf16,
        choice,
        partial,
        *others,
        b_maps,
    )
    return finish(un, over_z(out), base, ctx, own)


def solution(mesh):
    return jax.shard_map(
        body,
        mesh=mesh,
        in_specs=(
            P("rows", None),
            P(None, "tp"),
            P("rows", "tp", None),
            P("rows", None, "tp"),
            P(),
            P(),
            P("rows", None),
            P("rows", None),
            P("rows", "tp"),
            P("rows", "tp"),
            P("rows", None, "tp"),
            P("rows", None, "tp"),
        ),
        out_specs=(P("rows", "tp"), P("rows", "tp")),
        check_vma=False,
    )
```

```python
import functools
import math

import jax
import jax.numpy as jnp
from jax import lax
from jax.experimental import pallas as pl
from jax.experimental.pallas import tpu as pltpu
from jax.sharding import PartitionSpec as P

HEAD = 128
PLANE = 8
MOST = 8
f32 = jnp.float32
bf16 = jnp.bfloat16
i32 = jnp.int32
NT = (((1,), (1,)), ((), ()))
MIB = 1024 * 1024


FREE = pl.CostEstimate(flops=0, bytes_accessed=0, transcendentals=0)


def params(mib=12):
    return pltpu.CompilerParams(vmem_limit_bytes=mib * MIB)


def iota(shape, dim):
    return lax.broadcasted_iota(i32, shape, dim)


def segment_rows(meta):
    slots, groups = meta.slots, meta.groups
    adapters = meta.adapters
    listed = meta.ref[pl.ds(lax.axis_index("rows"), 1), :slots]
    hit = (iota((adapters, slots), 0) == listed).astype(f32)
    table = jnp.broadcast_to(meta.table().astype(f32), (8, adapters))
    position = jnp.dot(table, hit, preferred_element_type=f32)[:1]
    owner = jnp.right_shift(position.astype(i32), 1).astype(f32)
    lens = meta.ref[groups + 1 : groups + 2, :slots].astype(f32)
    before = (iota((slots, slots), 0) < iota((slots, slots), 1)).astype(f32)
    start = jnp.dot(jnp.broadcast_to(lens, (8, slots)), before, preferred_element_type=f32)[:1]
    return owner, start, lens


class Meta:
    def __init__(self, ref, groups, slots, adapters):
        self.ref, self.groups, self.slots, self.adapters = ref, groups, slots, adapters

    def table(self):
        return self.ref[self.groups : self.groups + 1, : self.adapters]


def ahead(q):
    i = jnp.right_shift(q, 1)
    odd = jnp.bitwise_and(q, 1) == 1
    return jnp.where(odd, jnp.where(i == 0, 4, 8 - i), i)


def slot_owner(slot, plane):
    z = lax.div(lax.axis_index("rows"), plane)
    q = jnp.bitwise_and(jnp.right_shift(slot, 3), 7)
    return jnp.bitwise_and(z + ahead(q), 7) * plane + jnp.right_shift(slot, 6)


def place_kernel(plane, sizes, meta_ref, x_ref, out_ref, token_ref):
    count = out_ref.shape[0]
    rows = x_ref.shape[0]
    token_ref[...] = jnp.zeros_like(token_ref)
    owner, start, lengths = segment_rows(Meta(meta_ref, *sizes))
    slot = iota((count, 1), 0)
    mine = owner == slot_owner(slot, plane).astype(f32)
    begin = jnp.sum(jnp.where(mine, start, 0.0), axis=1, keepdims=True)
    length = jnp.sum(jnp.where(mine, lengths, 0.0), axis=1, keepdims=True)
    within = jnp.bitwise_and(slot, MOST - 1).astype(f32)
    source = jnp.where(within < length, begin + within, -1.0)
    placing = (iota((count, rows), 1).astype(f32) == source).astype(bf16)
    out_ref[...] = jnp.dot(placing, x_ref[...], preferred_element_type=f32).astype(bf16)


def place(sizes, meta, x_part, count):
    part = x_part.shape[1]
    vmem = pl.BlockSpec(memory_space=pltpu.VMEM)
    return pl.pallas_call(
        functools.partial(place_kernel, PLANE, sizes),
        out_shape=(
            jax.ShapeDtypeStruct((count, part), bf16),
            jax.ShapeDtypeStruct((8, 128), i32),
        ),
        in_specs=[vmem, vmem],
        out_specs=(vmem, vmem),
        compiler_params=params(),
    )(meta, x_part)


def unplace_kernel(plane, sizes, meta_ref, token_ref, out_ref):
    rows, count = out_ref.shape
    owner, start, lens = segment_rows(Meta(meta_ref, *sizes))
    row = iota((rows, 1), 0).astype(f32)
    inside = (row >= start) & (row < start + lens)
    target = jnp.sum(jnp.where(inside, owner * MOST + row - start, 0.0), axis=1, keepdims=True)
    slot = iota((1, count), 1)
    meant = slot_owner(slot, plane) * MOST + jnp.bitwise_and(slot, MOST - 1)
    out_ref[...] = (meant.astype(f32) == target).astype(bf16)


def choose_kernel(plane, sizes, meta_ref, token_ref, out_ref):
    meta = Meta(meta_ref, *sizes)
    count = out_ref.shape[0]
    rows = lax.axis_index("rows")
    z, at = lax.div(rows, plane), lax.rem(rows, plane)
    listed = meta_ref[pl.ds(pl.multiple_of(z * plane, plane), plane), : meta.slots]
    table = meta.table()
    ids = iota((1, meta.adapters), 1)
    lane = iota((plane, 128), 1)
    uses = jnp.zeros((plane, 128), f32)
    for q in range(8):
        step = (0, 4, 1, 7, 2, 6, 3, 5)[q]
        owner = jnp.bitwise_and(z + step, 7) * plane + at
        second = jnp.max(jnp.where(table == 2 * owner + 1, ids, -1), axis=1, keepdims=True)
        hit = jnp.max((listed == second).astype(f32), axis=1, keepdims=True)
        uses = jnp.where(lane == q, hit, uses)
    row = iota((count, 1), 0)
    both = 2 * MOST
    q_of = lax.div(row, both * plane) * 2 + jnp.bitwise_and(jnp.right_shift(row, 3), 1)
    source = lax.rem(lax.div(row, both), plane)
    spread = (source == iota((count, plane), 1)).astype(f32)
    wide = jnp.dot(spread, uses, preferred_element_type=f32)
    mine = iota((count, 128), 1) == q_of
    out_ref[...] = jnp.broadcast_to(
        jnp.sum(jnp.where(mine, wide, 0.0), axis=1, keepdims=True), out_ref.shape
    )


def pair_rows(x_ref, pair):
    tile = 2 * MOST
    return jnp.concatenate(
        [x_ref[at : at + tile, :] for at in range(pair * tile, x_ref.shape[0], 8 * MOST)], axis=0
    )


def turn(low, second):
    turned = pltpu.roll(low, low.shape[1] // 2, 1)
    return jnp.where(second, turned, low), jnp.where(second, low, turned)


def early_kernel(choice_ref, x_ref, own_ref, d1, u1, d2, u2, d3, u3, out_ref, kept_ref):
    part = x_ref.shape[1]
    many, both = out_ref.shape[0] // 2, out_ref.shape[1]
    odd = jnp.bitwise_and(iota((many, both), 0), MOST) > 0
    second = [choice_ref[i * many : (i + 1) * many, :] > 0.5 for i in range(4)]
    kept = pair_rows(x_ref, 0)
    kept_ref[...] = kept
    sides = [turn(jnp.dot(kept, own_ref[:part], preferred_element_type=f32), second[0])]
    for i, (even_map, odd_map) in enumerate(((d1, u1), (d2, u2), (d3, u3))):
        a = jnp.concatenate([even_map[:part], odd_map[:part]], axis=1)
        each = jnp.dot(pair_rows(x_ref, i + 1), a, preferred_element_type=f32)
        sides.append(turn(jnp.where(odd, each[:, both:], each[:, :both]), second[i + 1]))
    left = iota((many, both), 1) < both // 2
    out_ref[:many] = jnp.where(left, sides[0][0], sides[2][1])
    out_ref[many:] = jnp.where(left, sides[1][0], sides[3][1])


def final_kernel(choice_ref, kept_ref, a_ref, b_ref, early_ref, out_ref):
    many, part = kept_ref.shape
    both = out_ref.shape[1]
    cut = a_ref.shape[0]
    low = jnp.dot(kept_ref[:, :cut], a_ref[...], preferred_element_type=f32)
    low = low + jnp.dot(kept_ref[:, cut:], b_ref[: part - cut], preferred_element_type=f32)
    low = turn(low, choice_ref[:many, :] > 0.5)[0]
    odd = jnp.bitwise_and(iota((many, both), 0), MOST) > 0
    mine = odd & (iota((many, both), 1) < both // 2)
    out_ref[:many] = jnp.where(mine, low, early_ref[:many])
    out_ref[many:] = early_ref[many:]


def delta_kernel(choice_ref, p0, p1, p2, p3, own, last, d1, u1, d2, u2, d3, u3, out_ref):
    count, width = out_ref.shape
    half, both = p0.shape
    rank = both // 2
    tile = 2 * MOST
    low = (p0[...] + p1[...]) + (p2[...] + p3[...])
    turned = pltpu.roll(low, rank, 1)
    lane = iota((half, both), 1) < rank
    twice = jnp.concatenate([jnp.where(lane, low, turned), jnp.where(lane, turned, low)], axis=0)
    keep = (iota((count, both), 1) >= rank) == (choice_ref[...] > 0.5)
    low = jnp.where(keep, twice, 0.0)
    odd = jnp.bitwise_and(iota((count, both), 0), MOST) > 0
    spread = jnp.concatenate(
        [jnp.where(odd, 0.0, low), jnp.where(odd, low, 0.0)], axis=1
    ).astype(bf16)
    many = count // 4
    for pair, refs in enumerate(((own, last), (d1, u1), (d2, u2), (d3, u3))):
        wide = []
        for ref in refs:
            first = ref.shape[0] - width
            wide.append(
                jnp.concatenate(
                    [ref[first + at : first + at + both] for at in range(0, width, both)], axis=1
                )
            )
        got = jnp.dot(
            spread[pair * many : (pair + 1) * many],
            jnp.concatenate(wide, axis=0),
            preferred_element_type=f32,
        ).astype(bf16)
        for i in range(many // tile):
            at = i * 8 * MOST + pair * tile
            out_ref[at : at + tile, :] = got[i * tile : (i + 1) * tile]


def vmem_spec():
    return pl.BlockSpec(memory_space=pltpu.VMEM)


def halves_kernel(a_ref, b_ref, a_out, b_out):
    a_out[...] = a_ref[...]
    b_out[...] = b_ref[...]


def halves(a, b):
    shape = (a.shape[0] // 2, a.shape[1])
    return pl.pallas_call(
        halves_kernel,
        out_shape=(jax.ShapeDtypeStruct(shape, a.dtype),) * 2,
        grid=(1,),
        in_specs=[pl.BlockSpec(shape, lambda i: (0, 0)), pl.BlockSpec(shape, lambda i: (1, 0))],
        out_specs=(pl.BlockSpec(shape, lambda i: (0, 0)),) * 2,
        cost_estimate=FREE,
        compiler_params=params(),
    )(a, b)


def delta_call(choice, parts, maps, count, width):
    def whole(a):
        return pl.BlockSpec(a.shape, lambda i: (0, 0))

    def tail(a):
        last = a.shape[0] // width - 1
        return pl.BlockSpec((width, a.shape[1]), lambda i: (last, 0))

    return pl.pallas_call(
        delta_kernel,
        out_shape=jax.ShapeDtypeStruct((count, width), bf16),
        grid=(1,),
        in_specs=[whole(a) for a in (choice, *parts)]
        + [tail(a) if a.shape[0] % width == 0 else whole(a) for a in maps],
        out_specs=pl.BlockSpec((count, width), lambda i: (0, 0)),
        compiler_params=params(),
    )(choice, *parts, *maps)


def vmem_call(kernel, outs, *args):
    return pl.pallas_call(
        kernel,
        out_shape=tuple(jax.ShapeDtypeStruct(shape, dtype) for shape, dtype in outs),
        in_specs=[vmem_spec()] * len(args),
        out_specs=(vmem_spec(),) * len(outs),
        cost_estimate=FREE,
        compiler_params=params(),
    )(*args)


def attend_kernel(scale, q_ref, nk_ref, k_ref, v_ref, len_ref, *refs):
    ctx_ref, own_ref = refs[-2:]
    rows, cache, width = k_ref.shape
    kv_heads = width // HEAD
    group = q_ref.shape[1] // width
    many = 8 * group
    row = jnp.bitwise_and(iota((many, 128), 0), 7)
    lane = iota((many, 128), 1)
    upper = row >= 4
    place_ok = jnp.right_shift(lane, 5) == jnp.bitwise_and(row, 3)
    cell = jnp.bitwise_and(lane, cache - 1)
    lane8 = iota((8, 128), 1)
    for pair in range(rows // 16):
        q16 = q_ref[pl.ds(pair * 16, 16), :].astype(f32)
        nk16 = nk_ref[pl.ds(pair * 16, 16), :].astype(f32)
        for sub in range(2):
            base = pair * 16 + sub * 8
            q8 = q16[sub * 8 : sub * 8 + 8]
            nk8 = nk16[sub * 8 : sub * 8 + 8]
            keys = k_ref[pl.ds(base, 8)].reshape(8 * cache, width)
            values = v_ref[pl.ds(base, 8)].reshape(8 * cache, width)
            lens = jnp.concatenate([len_ref[pl.ds(base, 8), :]] * group, axis=0)
            valid = place_ok & (cell < lens)
            own_tile = jnp.zeros((8, 128), f32)
            for h in range(kv_heads):
                cut = slice(h * HEAD, (h + 1) * HEAD)
                q = jnp.concatenate(
                    [q8[:, (h * group + g) * HEAD : (h * group + g + 1) * HEAD] for g in range(group)],
                    axis=0,
                )
                score = lax.dot_general(
                    q.astype(bf16), keys[:, cut], NT, preferred_element_type=f32
                )
                score = jnp.where(upper, score[:, 128:], score[:, :128]) * scale
                score = jnp.where(valid, score, -1e30)
                own = jnp.sum(
                    q * jnp.concatenate([nk8[:, cut]] * group, axis=0), axis=1, keepdims=True
                ) * scale
                top = jnp.maximum(jnp.max(score, axis=1, keepdims=True), own)
                weight = jnp.where(valid, jnp.exp(score - top), 0.0)
                e_own = jnp.exp(own - top)
                inv = 1.0 / (jnp.sum(weight, axis=1, keepdims=True) + e_own)
                split = jnp.concatenate(
                    [jnp.where(upper, 0.0, weight), jnp.where(upper, weight, 0.0)], axis=1
                ).astype(bf16)
                ctx = jnp.dot(split, values[:, cut], preferred_element_type=f32) * inv
                w_own = e_own.astype(bf16).astype(f32) * inv
                for g in range(group):
                    head = h * group + g
                    ctx_ref[pl.ds(base, 8), head * HEAD : (head + 1) * HEAD] = ctx[g * 8 : g * 8 + 8]
                    own_tile = jnp.where(lane8 == head, w_own[g * 8 : g * 8 + 8], own_tile)
            own_ref[pl.ds(base, 8), :] = own_tile


def attend(first, steps, queries, new_key, cache_keys, cache_values, lengths, before=()):
    rows, wide = queries.shape
    cache, width = cache_keys.shape[1:]
    step = 32
    return pl.pallas_call(
        functools.partial(attend_kernel, 1.0 / math.sqrt(HEAD)),
        out_shape=(
            jax.ShapeDtypeStruct((rows, wide), f32),
            jax.ShapeDtypeStruct((rows, 128), f32),
        ),
        grid=(steps,),
        in_specs=[
            pl.BlockSpec((step, wide), lambda i: (i + first, 0)),
            pl.BlockSpec((step, width), lambda i: (i + first, 0)),
            pl.BlockSpec((step, cache, width), lambda i: (i + first, 0, 0)),
            pl.BlockSpec((step, cache, width), lambda i: (i + first, 0, 0)),
            pl.BlockSpec((step, 1), lambda i: (i + first, 0)),
        ]
        + [pl.BlockSpec(memory_space=pl.ANY)] * len(before),
        out_specs=(
            pl.BlockSpec((step, wide), lambda i: (i + first, 0)),
            pl.BlockSpec((step, 128), lambda i: (i + first, 0)),
        ),
        input_output_aliases={5 + i: i for i in range(len(before))},
        cost_estimate=FREE,
        compiler_params=params(60),
    )(queries, new_key, cache_keys, cache_values, lengths, *before)


def finish_kernel(un_ref, delta_ref, base_ref, ctx_ref, own_ref, value_ref, out_ref):
    heads = out_ref.shape[1] // HEAD
    group = out_ref.shape[1] // value_ref.shape[1]
    delta = jnp.dot(un_ref[...], delta_ref[...], preferred_element_type=f32)
    value = (base_ref[...] + delta).astype(bf16)
    value_ref[...] = value
    value = value.astype(f32)
    for head in range(heads):
        kv = head // group
        cut = slice(head * HEAD, (head + 1) * HEAD)
        out_ref[:, cut] = (
            ctx_ref[:, cut] + own_ref[:, head : head + 1] * value[:, kv * HEAD : (kv + 1) * HEAD]
        ).astype(bf16)


def finish(un, delta, base, ctx, own):
    rows, wide = ctx.shape
    step = 64
    by_row = lambda n: pl.BlockSpec((step, n), lambda i: (i, 0))
    whole = lambda a: pl.BlockSpec(a.shape, lambda i: (0, 0))
    return pl.pallas_call(
        finish_kernel,
        out_shape=(
            jax.ShapeDtypeStruct(base.shape, bf16),
            jax.ShapeDtypeStruct((rows, wide), bf16),
        ),
        grid=(rows // step,),
        in_specs=[
            by_row(un.shape[1]),
            whole(delta),
            by_row(base.shape[1]),
            by_row(wide),
            by_row(128),
        ],
        out_specs=(by_row(base.shape[1]), by_row(wide)),
        compiler_params=params(),
    )(un, delta, base, ctx, own)


def body(
    normed_rows,
    value_weight,
    adapter_a,
    adapter_b,
    page_table,
    group_list,
    seg_len,
    kv_len,
    queries,
    new_key,
    cache_keys,
    cache_values,
):
    tp = lax.axis_size("tp")
    groups = lax.axis_size("rows")
    planes = groups // PLANE
    rows = normed_rows.shape[0]
    part = normed_rows.shape[1] // tp
    per_owner, _, rank = adapter_a.shape
    width = adapter_b.shape[2]
    count = groups * MOST
    slots, adapters = group_list.shape[1], page_table.shape[0]
    sizes = (groups, slots, adapters)
    wide = lambda x: jnp.pad(x, ((0, 0), (0, 128 - x.shape[1])))
    meta = jnp.concatenate([wide(group_list), wide(page_table.reshape(1, -1)), wide(seg_len)], axis=0)
    planes_of = [[z * PLANE + at for at in range(PLANE)] for z in range(planes)]
    both = per_owner * rank
    lengths = kv_len.reshape(-1, 1)

    def shift_z(x, by):
        return lax.ppermute(
            x, "rows", [(r, (r + by * PLANE) % groups) for r in range(groups)]
        )

    def over_plane(x):
        size, wide = x.shape
        x = lax.all_to_all(
            x.reshape(PLANE, size // PLANE, wide),
            "rows",
            split_axis=0,
            concat_axis=0,
            axis_index_groups=planes_of,
            tiled=True,
        )
        return x.reshape(size, wide)

    packed = jnp.concatenate(
        [jnp.swapaxes(adapter_a, 0, 1).reshape(part, both)]
        + [adapter_b.reshape(both, width)[:, at : at + both] for at in range(0, width, both)],
        axis=0,
    )
    up, down = [shift_z(packed, 1)], [shift_z(packed, -1)]

    packed, normed_rows, meta = lax.optimization_barrier((packed, normed_rows, meta))
    x_part = lax.dynamic_slice_in_dim(normed_rows, lax.axis_index("tp") * part, part, 1)
    placed, token = place(sizes, meta, x_part, count)
    arrived = over_plane(placed)
    (choice,) = vmem_call(
        functools.partial(choose_kernel, PLANE, sizes), [((count, both), f32)], meta, token
    )
    up[0], choice, lengths = lax.optimization_barrier((up[0], choice, lengths))
    up.append(shift_z(up[0], 1))
    down[0], choice, lengths = lax.optimization_barrier((down[0], choice, lengths))
    down.append(shift_z(down[0], -1))
    up[0], down[0], queries = lax.optimization_barrier((up[0], down[0], queries))
    steps = rows // 64
    done = attend(0, steps, queries, new_key, cache_keys, cache_values, lengths)
    up[1], done = lax.optimization_barrier((up[1], done))
    up.append(shift_z(up[1], 1))
    down[1], done = lax.optimization_barrier((down[1], done))
    down.append(shift_z(down[1], -1))
    up[1], down[1], queries = lax.optimization_barrier((up[1], down[1], queries))
    ctx, own = attend(steps, steps, queries, new_key, cache_keys, cache_values, lengths, done)
    up[2], down[2], ctx, own, meta = lax.optimization_barrier((up[2], down[2], ctx, own, meta))
    half_up, half_down = halves(up[2], down[2])
    last_a, last_b = shift_z(half_up, 1), shift_z(half_down, -1)
    (un,) = vmem_call(
        functools.partial(unplace_kernel, PLANE, sizes), [((rows, count), bf16)], meta, token
    )
    maps = [m for pair in zip(down, up) for m in pair]
    early, kept = vmem_call(
        early_kernel,
        [((count // 2, both), f32), ((count // 4, part), bf16)],
        choice,
        arrived,
        packed,
        *maps,
    )
    last_a, last_b, early, kept, un = lax.optimization_barrier((last_a, last_b, early, kept, un))
    (partial,) = vmem_call(
        final_kernel, [((count // 2, both), f32)], choice, kept, last_a, last_b, early
    )
    others = [
        lax.ppermute(partial, "tp", [(j, (j + k) % tp) for j in range(tp)]) for k in range(1, tp)
    ]
    partial, normed_rows = lax.optimization_barrier((partial, normed_rows))
    base = jnp.dot(normed_rows, value_weight, preferred_element_type=f32)
    *others, base = lax.optimization_barrier((*others, base))
    out = delta_call(choice, [partial, *others], [packed, last_b, *maps], count, width)
    return finish(un, over_plane(out), base, ctx, own)


def solution(mesh):
    return jax.shard_map(
        body,
        mesh=mesh,
        in_specs=(
            P("rows", None),
            P(None, "tp"),
            P("rows", "tp", None),
            P("rows", None, "tp"),
            P(),
            P(),
            P("rows", None),
            P("rows", None),
            P("rows", "tp"),
            P("rows", "tp"),
            P("rows", None, "tp"),
            P("rows", None, "tp"),
        ),
        out_specs=(P("rows", "tp"), P("rows", "tp")),
        check_vma=False,
    )
```

```python
import functools
import math

import jax
import jax.numpy as jnp
from jax import lax
from jax.experimental import pallas as pl
from jax.experimental.pallas import tpu as pltpu
from jax.sharding import PartitionSpec as P

HEAD = 128
PLANE = 8
MOST = 8
f32 = jnp.float32
bf16 = jnp.bfloat16
i32 = jnp.int32
NT = (((1,), (1,)), ((), ()))
MIB = 1024 * 1024


FREE = pl.CostEstimate(flops=0, bytes_accessed=0, transcendentals=0)


def params(mib=12):
    return pltpu.CompilerParams(vmem_limit_bytes=mib * MIB)


def iota(shape, dim):
    return lax.broadcasted_iota(i32, shape, dim)


def segment_rows(meta):
    slots, groups = meta.slots, meta.groups
    adapters = meta.adapters
    listed = meta.ref[pl.ds(lax.axis_index("rows"), 1), :slots]
    hit = (iota((adapters, slots), 0) == listed).astype(f32)
    table = jnp.broadcast_to(meta.table().astype(f32), (8, adapters))
    position = jnp.dot(table, hit, preferred_element_type=f32)[:1]
    owner = jnp.right_shift(position.astype(i32), 1).astype(f32)
    lens = meta.ref[groups + 1 : groups + 2, :slots].astype(f32)
    before = (iota((slots, slots), 0) < iota((slots, slots), 1)).astype(f32)
    start = jnp.dot(jnp.broadcast_to(lens, (8, slots)), before, preferred_element_type=f32)[:1]
    return owner, start, lens


class Meta:
    def __init__(self, ref, groups, slots, adapters):
        self.ref, self.groups, self.slots, self.adapters = ref, groups, slots, adapters

    def table(self):
        return self.ref[self.groups : self.groups + 1, : self.adapters]


def ahead(q):
    i = jnp.right_shift(q, 1)
    odd = jnp.bitwise_and(q, 1) == 1
    return jnp.where(odd, jnp.where(i == 0, 4, 8 - i), i)


def slot_owner(slot, plane):
    z = lax.div(lax.axis_index("rows"), plane)
    q = jnp.bitwise_and(jnp.right_shift(slot, 3), 7)
    return jnp.bitwise_and(z + ahead(q), 7) * plane + jnp.right_shift(slot, 6)


def place_kernel(plane, sizes, meta_ref, x_ref, out_ref, token_ref):
    count = out_ref.shape[0]
    rows = x_ref.shape[0]
    token_ref[...] = jnp.zeros_like(token_ref)
    owner, start, lengths = segment_rows(Meta(meta_ref, *sizes))
    slot = iota((count, 1), 0)
    mine = owner == slot_owner(slot, plane).astype(f32)
    begin = jnp.sum(jnp.where(mine, start, 0.0), axis=1, keepdims=True)
    length = jnp.sum(jnp.where(mine, lengths, 0.0), axis=1, keepdims=True)
    within = jnp.bitwise_and(slot, MOST - 1).astype(f32)
    source = jnp.where(within < length, begin + within, -1.0)
    placing = (iota((count, rows), 1).astype(f32) == source).astype(bf16)
    out_ref[...] = jnp.dot(placing, x_ref[...], preferred_element_type=f32).astype(bf16)


def place(sizes, meta, x_part, count):
    part = x_part.shape[1]
    vmem = pl.BlockSpec(memory_space=pltpu.VMEM)
    return pl.pallas_call(
        functools.partial(place_kernel, PLANE, sizes),
        out_shape=(
            jax.ShapeDtypeStruct((count, part), bf16),
            jax.ShapeDtypeStruct((8, 128), i32),
        ),
        in_specs=[vmem, vmem],
        out_specs=(vmem, vmem),
        compiler_params=params(),
    )(meta, x_part)


def unplace_kernel(plane, sizes, meta_ref, token_ref, out_ref):
    rows, count = out_ref.shape
    owner, start, lens = segment_rows(Meta(meta_ref, *sizes))
    row = iota((rows, 1), 0).astype(f32)
    inside = (row >= start) & (row < start + lens)
    target = jnp.sum(jnp.where(inside, owner * MOST + row - start, 0.0), axis=1, keepdims=True)
    slot = iota((1, count), 1)
    meant = slot_owner(slot, plane) * MOST + jnp.bitwise_and(slot, MOST - 1)
    out_ref[...] = (meant.astype(f32) == target).astype(bf16)


def choose_kernel(plane, sizes, meta_ref, token_ref, out_ref):
    meta = Meta(meta_ref, *sizes)
    count = out_ref.shape[0]
    rows = lax.axis_index("rows")
    z, at = lax.div(rows, plane), lax.rem(rows, plane)
    listed = meta_ref[pl.ds(pl.multiple_of(z * plane, plane), plane), : meta.slots]
    table = meta.table()
    ids = iota((1, meta.adapters), 1)
    lane = iota((plane, 128), 1)
    uses = jnp.zeros((plane, 128), f32)
    for q in range(8):
        step = (0, 4, 1, 7, 2, 6, 3, 5)[q]
        owner = jnp.bitwise_and(z + step, 7) * plane + at
        second = jnp.max(jnp.where(table == 2 * owner + 1, ids, -1), axis=1, keepdims=True)
        hit = jnp.max((listed == second).astype(f32), axis=1, keepdims=True)
        uses = jnp.where(lane == q, hit, uses)
    row = iota((count, 1), 0)
    both = 2 * MOST
    q_of = lax.div(row, both * plane) * 2 + jnp.bitwise_and(jnp.right_shift(row, 3), 1)
    source = lax.rem(lax.div(row, both), plane)
    spread = (source == iota((count, plane), 1)).astype(f32)
    wide = jnp.dot(spread, uses, preferred_element_type=f32)
    mine = iota((count, 128), 1) == q_of
    out_ref[...] = jnp.broadcast_to(
        jnp.sum(jnp.where(mine, wide, 0.0), axis=1, keepdims=True), out_ref.shape
    )


def pair_rows(x_ref, pair):
    tile = 2 * MOST
    return jnp.concatenate(
        [x_ref[at : at + tile, :] for at in range(pair * tile, x_ref.shape[0], 8 * MOST)], axis=0
    )


def turn(low, second):
    turned = pltpu.roll(low, low.shape[1] // 2, 1)
    return jnp.where(second, turned, low), jnp.where(second, low, turned)


def early_kernel(choice_ref, x_ref, own_ref, d1, u1, d2, u2, d3, u3, out_ref, kept_ref):
    part = x_ref.shape[1]
    many, both = out_ref.shape[0] // 2, out_ref.shape[1]
    odd = jnp.bitwise_and(iota((many, both), 0), MOST) > 0
    second = [choice_ref[i * many : (i + 1) * many, :] > 0.5 for i in range(4)]
    kept = pair_rows(x_ref, 0)
    kept_ref[...] = kept
    sides = [turn(jnp.dot(kept, own_ref[:part], preferred_element_type=f32), second[0])]
    for i, (even_map, odd_map) in enumerate(((d1, u1), (d2, u2), (d3, u3))):
        a = jnp.concatenate([even_map[:part], odd_map[:part]], axis=1)
        each = jnp.dot(pair_rows(x_ref, i + 1), a, preferred_element_type=f32)
        sides.append(turn(jnp.where(odd, each[:, both:], each[:, :both]), second[i + 1]))
    left = iota((many, both), 1) < both // 2
    out_ref[:many] = jnp.where(left, sides[0][0], sides[2][1])
    out_ref[many:] = jnp.where(left, sides[1][0], sides[3][1])


def final_kernel(choice_ref, kept_ref, a_ref, b_ref, early_ref, out_ref):
    many, part = kept_ref.shape
    both = out_ref.shape[1]
    cut = a_ref.shape[0]
    low = jnp.dot(kept_ref[:, :cut], a_ref[...], preferred_element_type=f32)
    low = low + jnp.dot(kept_ref[:, cut:], b_ref[: part - cut], preferred_element_type=f32)
    low = turn(low, choice_ref[:many, :] > 0.5)[0]
    odd = jnp.bitwise_and(iota((many, both), 0), MOST) > 0
    mine = odd & (iota((many, both), 1) < both // 2)
    out_ref[:many] = jnp.where(mine, low, early_ref[:many])
    out_ref[many:] = early_ref[many:]


def delta_kernel(choice_ref, p0, p1, p2, p3, own, last, d1, u1, d2, u2, d3, u3, out_ref):
    count, width = out_ref.shape
    half, both = p0.shape
    rank = both // 2
    tile = 2 * MOST
    low = (p0[...] + p1[...]) + (p2[...] + p3[...])
    turned = pltpu.roll(low, rank, 1)
    lane = iota((half, both), 1) < rank
    twice = jnp.concatenate([jnp.where(lane, low, turned), jnp.where(lane, turned, low)], axis=0)
    keep = (iota((count, both), 1) >= rank) == (choice_ref[...] > 0.5)
    low = jnp.where(keep, twice, 0.0)
    odd = jnp.bitwise_and(iota((count, both), 0), MOST) > 0
    spread = jnp.concatenate(
        [jnp.where(odd, 0.0, low), jnp.where(odd, low, 0.0)], axis=1
    ).astype(bf16)
    many = count // 4
    for pair, refs in enumerate(((own, last), (d1, u1), (d2, u2), (d3, u3))):
        wide = []
        for ref in refs:
            first = ref.shape[0] - width
            wide.append(
                jnp.concatenate(
                    [ref[first + at : first + at + both] for at in range(0, width, both)], axis=1
                )
            )
        got = jnp.dot(
            spread[pair * many : (pair + 1) * many],
            jnp.concatenate(wide, axis=0),
            preferred_element_type=f32,
        ).astype(bf16)
        for i in range(many // tile):
            at = i * 8 * MOST + pair * tile
            out_ref[at : at + tile, :] = got[i * tile : (i + 1) * tile]


def vmem_spec():
    return pl.BlockSpec(memory_space=pltpu.VMEM)


def halves_kernel(a_ref, b_ref, a_out, b_out):
    a_out[...] = a_ref[...]
    b_out[...] = b_ref[...]


def halves(a, b):
    shape = (a.shape[0] // 2, a.shape[1])
    return pl.pallas_call(
        halves_kernel,
        out_shape=(jax.ShapeDtypeStruct(shape, a.dtype),) * 2,
        grid=(1,),
        in_specs=[pl.BlockSpec(shape, lambda i: (0, 0)), pl.BlockSpec(shape, lambda i: (1, 0))],
        out_specs=(pl.BlockSpec(shape, lambda i: (0, 0)),) * 2,
        cost_estimate=FREE,
        compiler_params=params(),
    )(a, b)


def delta_call(choice, parts, maps, count, width):
    def whole(a):
        return pl.BlockSpec(a.shape, lambda i: (0, 0))

    def tail(a):
        last = a.shape[0] // width - 1
        return pl.BlockSpec((width, a.shape[1]), lambda i: (last, 0))

    return pl.pallas_call(
        delta_kernel,
        out_shape=jax.ShapeDtypeStruct((count, width), bf16),
        grid=(1,),
        in_specs=[whole(a) for a in (choice, *parts)]
        + [tail(a) if a.shape[0] % width == 0 else whole(a) for a in maps],
        out_specs=pl.BlockSpec((count, width), lambda i: (0, 0)),
        compiler_params=params(),
    )(choice, *parts, *maps)


def vmem_call(kernel, outs, *args):
    return pl.pallas_call(
        kernel,
        out_shape=tuple(jax.ShapeDtypeStruct(shape, dtype) for shape, dtype in outs),
        in_specs=[vmem_spec()] * len(args),
        out_specs=(vmem_spec(),) * len(outs),
        cost_estimate=FREE,
        compiler_params=params(),
    )(*args)


def attend_kernel(scale, q_ref, nk_ref, k_ref, v_ref, len_ref, *refs):
    ctx_ref, own_ref = refs[-2:]
    rows, cache, width = k_ref.shape
    kv_heads = width // HEAD
    group = q_ref.shape[1] // width
    many = 8 * group
    row = jnp.bitwise_and(iota((many, 128), 0), 7)
    lane = iota((many, 128), 1)
    upper = row >= 4
    place_ok = jnp.right_shift(lane, 5) == jnp.bitwise_and(row, 3)
    cell = jnp.bitwise_and(lane, cache - 1)
    lane8 = iota((8, 128), 1)
    for pair in range(rows // 16):
        q16 = q_ref[pl.ds(pair * 16, 16), :].astype(f32)
        nk16 = nk_ref[pl.ds(pair * 16, 16), :].astype(f32)
        for sub in range(2):
            base = pair * 16 + sub * 8
            q8 = q16[sub * 8 : sub * 8 + 8]
            nk8 = nk16[sub * 8 : sub * 8 + 8]
            keys = k_ref[pl.ds(base, 8)].reshape(8 * cache, width)
            values = v_ref[pl.ds(base, 8)].reshape(8 * cache, width)
            lens = jnp.concatenate([len_ref[pl.ds(base, 8), :]] * group, axis=0)
            valid = place_ok & (cell < lens)
            own_tile = jnp.zeros((8, 128), f32)
            for h in range(kv_heads):
                cut = slice(h * HEAD, (h + 1) * HEAD)
                q = jnp.concatenate(
                    [q8[:, (h * group + g) * HEAD : (h * group + g + 1) * HEAD] for g in range(group)],
                    axis=0,
                )
                score = lax.dot_general(
                    q.astype(bf16), keys[:, cut], NT, preferred_element_type=f32
                )
                score = jnp.where(upper, score[:, 128:], score[:, :128]) * scale
                score = jnp.where(valid, score, -1e30)
                own = jnp.sum(
                    q * jnp.concatenate([nk8[:, cut]] * group, axis=0), axis=1, keepdims=True
                ) * scale
                top = jnp.maximum(jnp.max(score, axis=1, keepdims=True), own)
                weight = jnp.where(valid, jnp.exp(score - top), 0.0)
                e_own = jnp.exp(own - top)
                inv = 1.0 / (jnp.sum(weight, axis=1, keepdims=True) + e_own)
                split = jnp.concatenate(
                    [jnp.where(upper, 0.0, weight), jnp.where(upper, weight, 0.0)], axis=1
                ).astype(bf16)
                ctx = jnp.dot(split, values[:, cut], preferred_element_type=f32) * inv
                w_own = e_own.astype(bf16).astype(f32) * inv
                for g in range(group):
                    head = h * group + g
                    ctx_ref[pl.ds(base, 8), head * HEAD : (head + 1) * HEAD] = ctx[g * 8 : g * 8 + 8]
                    own_tile = jnp.where(lane8 == head, w_own[g * 8 : g * 8 + 8], own_tile)
            own_ref[pl.ds(base, 8), :] = own_tile


def attend(first, steps, queries, new_key, cache_keys, cache_values, lengths, before=()):
    rows, wide = queries.shape
    cache, width = cache_keys.shape[1:]
    step = 32
    return pl.pallas_call(
        functools.partial(attend_kernel, 1.0 / math.sqrt(HEAD)),
        out_shape=(
            jax.ShapeDtypeStruct((rows, wide), f32),
            jax.ShapeDtypeStruct((rows, 128), f32),
        ),
        grid=(steps,),
        in_specs=[
            pl.BlockSpec((step, wide), lambda i: (i + first, 0)),
            pl.BlockSpec((step, width), lambda i: (i + first, 0)),
            pl.BlockSpec((step, cache, width), lambda i: (i + first, 0, 0)),
            pl.BlockSpec((step, cache, width), lambda i: (i + first, 0, 0)),
            pl.BlockSpec((step, 1), lambda i: (i + first, 0)),
        ]
        + [pl.BlockSpec(memory_space=pl.ANY)] * len(before),
        out_specs=(
            pl.BlockSpec((step, wide), lambda i: (i + first, 0)),
            pl.BlockSpec((step, 128), lambda i: (i + first, 0)),
        ),
        input_output_aliases={5 + i: i for i in range(len(before))},
        cost_estimate=FREE,
        compiler_params=params(60),
    )(queries, new_key, cache_keys, cache_values, lengths, *before)


def finish_kernel(un_ref, delta_ref, base_ref, ctx_ref, own_ref, value_ref, out_ref):
    heads = out_ref.shape[1] // HEAD
    group = out_ref.shape[1] // value_ref.shape[1]
    delta = jnp.dot(un_ref[...], delta_ref[...], preferred_element_type=f32)
    value = (base_ref[...] + delta).astype(bf16)
    value_ref[...] = value
    value = value.astype(f32)
    for head in range(heads):
        kv = head // group
        cut = slice(head * HEAD, (head + 1) * HEAD)
        out_ref[:, cut] = (
            ctx_ref[:, cut] + own_ref[:, head : head + 1] * value[:, kv * HEAD : (kv + 1) * HEAD]
        ).astype(bf16)


def finish(un, delta, base, ctx, own):
    rows, wide = ctx.shape
    step = 128
    by_row = lambda n: pl.BlockSpec((step, n), lambda i: (i, 0))
    whole = lambda a: pl.BlockSpec(a.shape, lambda i: (0, 0))
    return pl.pallas_call(
        finish_kernel,
        out_shape=(
            jax.ShapeDtypeStruct(base.shape, bf16),
            jax.ShapeDtypeStruct((rows, wide), bf16),
        ),
        grid=(rows // step,),
        in_specs=[
            by_row(un.shape[1]),
            whole(delta),
            by_row(base.shape[1]),
            by_row(wide),
            by_row(128),
        ],
        out_specs=(by_row(base.shape[1]), by_row(wide)),
        compiler_params=params(),
    )(un, delta, base, ctx, own)


def body(
    normed_rows,
    value_weight,
    adapter_a,
    adapter_b,
    page_table,
    group_list,
    seg_len,
    kv_len,
    queries,
    new_key,
    cache_keys,
    cache_values,
):
    tp = lax.axis_size("tp")
    groups = lax.axis_size("rows")
    planes = groups // PLANE
    rows = normed_rows.shape[0]
    part = normed_rows.shape[1] // tp
    per_owner, _, rank = adapter_a.shape
    width = adapter_b.shape[2]
    count = groups * MOST
    slots, adapters = group_list.shape[1], page_table.shape[0]
    sizes = (groups, slots, adapters)
    wide = lambda x: jnp.pad(x, ((0, 0), (0, 128 - x.shape[1])))
    meta = jnp.concatenate([wide(group_list), wide(page_table.reshape(1, -1)), wide(seg_len)], axis=0)
    planes_of = [[z * PLANE + at for at in range(PLANE)] for z in range(planes)]
    both = per_owner * rank
    lengths = kv_len.reshape(-1, 1)

    def shift_z(x, by):
        return lax.ppermute(
            x, "rows", [(r, (r + by * PLANE) % groups) for r in range(groups)]
        )

    def over_plane(x):
        size, wide = x.shape
        x = lax.all_to_all(
            x.reshape(PLANE, size // PLANE, wide),
            "rows",
            split_axis=0,
            concat_axis=0,
            axis_index_groups=planes_of,
            tiled=True,
        )
        return x.reshape(size, wide)

    packed = jnp.concatenate(
        [jnp.swapaxes(adapter_a, 0, 1).reshape(part, both)]
        + [adapter_b.reshape(both, width)[:, at : at + both] for at in range(0, width, both)],
        axis=0,
    )
    up, down = [shift_z(packed, 1)], [shift_z(packed, -1)]

    packed, normed_rows, meta = lax.optimization_barrier((packed, normed_rows, meta))
    x_part = lax.dynamic_slice_in_dim(normed_rows, lax.axis_index("tp") * part, part, 1)
    placed, token = place(sizes, meta, x_part, count)
    arrived = over_plane(placed)
    (choice,) = vmem_call(
        functools.partial(choose_kernel, PLANE, sizes), [((count, both), f32)], meta, token
    )
    up[0], down[0], choice, queries, lengths = lax.optimization_barrier(
        (up[0], down[0], choice, queries, lengths)
    )
    up.append(shift_z(up[0], 1))
    down.append(shift_z(down[0], -1))
    steps = rows // 64
    done = attend(0, steps, queries, new_key, cache_keys, cache_values, lengths)
    up[1], down[1], done, queries = lax.optimization_barrier((up[1], down[1], done, queries))
    up.append(shift_z(up[1], 1))
    down.append(shift_z(down[1], -1))
    ctx, own = attend(steps, steps, queries, new_key, cache_keys, cache_values, lengths, done)
    up[2], down[2], ctx, own, meta = lax.optimization_barrier((up[2], down[2], ctx, own, meta))
    half_up, half_down = halves(up[2], down[2])
    last_a, last_b = shift_z(half_up, 1), shift_z(half_down, -1)
    (un,) = vmem_call(
        functools.partial(unplace_kernel, PLANE, sizes), [((rows, count), bf16)], meta, token
    )
    maps = [m for pair in zip(down, up) for m in pair]
    early, kept = vmem_call(
        early_kernel,
        [((count // 2, both), f32), ((count // 4, part), bf16)],
        choice,
        arrived,
        packed,
        *maps,
    )
    last_a, last_b, early, kept, un = lax.optimization_barrier((last_a, last_b, early, kept, un))
    (partial,) = vmem_call(
        final_kernel, [((count // 2, both), f32)], choice, kept, last_a, last_b, early
    )
    others = [
        lax.ppermute(partial, "tp", [(j, (j + k) % tp) for j in range(tp)]) for k in range(1, tp)
    ]
    partial, normed_rows = lax.optimization_barrier((partial, normed_rows))
    base = jnp.dot(normed_rows, value_weight, preferred_element_type=f32)
    *others, base = lax.optimization_barrier((*others, base))
    out = delta_call(choice, [partial, *others], [packed, last_b, *maps], count, width)
    return finish(un, over_plane(out), base, ctx, own)


def solution(mesh):
    return jax.shard_map(
        body,
        mesh=mesh,
        in_specs=(
            P("rows", None),
            P(None, "tp"),
            P("rows", "tp", None),
            P("rows", None, "tp"),
            P(),
            P(),
            P("rows", None),
            P("rows", None),
            P("rows", "tp"),
            P("rows", "tp"),
            P("rows", None, "tp"),
            P("rows", None, "tp"),
        ),
        out_specs=(P("rows", "tp"), P("rows", "tp")),
        check_vma=False,
    )
```

```python
import functools
import math

import jax
import jax.numpy as jnp
from jax import lax
from jax.experimental import pallas as pl
from jax.experimental.pallas import tpu as pltpu
from jax.sharding import PartitionSpec as P

HEAD = 128
PLANE = 8
MOST = 8
f32 = jnp.float32
bf16 = jnp.bfloat16
i32 = jnp.int32
NT = (((1,), (1,)), ((), ()))
MIB = 1024 * 1024


FREE = pl.CostEstimate(flops=0, bytes_accessed=0, transcendentals=0)


def params(mib=12):
    return pltpu.CompilerParams(vmem_limit_bytes=mib * MIB)


def iota(shape, dim):
    return lax.broadcasted_iota(i32, shape, dim)


def segment_rows(meta):
    slots, groups = meta.slots, meta.groups
    adapters = meta.adapters
    listed = meta.ref[pl.ds(lax.axis_index("rows"), 1), :slots]
    hit = (iota((adapters, slots), 0) == listed).astype(f32)
    table = jnp.broadcast_to(meta.table().astype(f32), (8, adapters))
    position = jnp.dot(table, hit, preferred_element_type=f32)[:1]
    owner = jnp.right_shift(position.astype(i32), 1).astype(f32)
    lens = meta.ref[groups + 1 : groups + 2, :slots].astype(f32)
    before = (iota((slots, slots), 0) < iota((slots, slots), 1)).astype(f32)
    start = jnp.dot(jnp.broadcast_to(lens, (8, slots)), before, preferred_element_type=f32)[:1]
    return owner, start, lens


class Meta:
    def __init__(self, ref, groups, slots, adapters):
        self.ref, self.groups, self.slots, self.adapters = ref, groups, slots, adapters

    def table(self):
        return self.ref[self.groups : self.groups + 1, : self.adapters]


def ahead(q):
    i = jnp.right_shift(q, 1)
    odd = jnp.bitwise_and(q, 1) == 1
    return jnp.where(odd, jnp.where(i == 0, 4, 8 - i), i)


def slot_owner(slot, plane):
    z = lax.div(lax.axis_index("rows"), plane)
    q = jnp.bitwise_and(jnp.right_shift(slot, 3), 7)
    return jnp.bitwise_and(z + ahead(q), 7) * plane + jnp.right_shift(slot, 6)


def place_kernel(plane, sizes, meta_ref, x_ref, out_ref, token_ref):
    count = out_ref.shape[0]
    rows = x_ref.shape[0]
    token_ref[...] = jnp.zeros_like(token_ref)
    owner, start, lengths = segment_rows(Meta(meta_ref, *sizes))
    slot = iota((count, 1), 0)
    mine = owner == slot_owner(slot, plane).astype(f32)
    begin = jnp.sum(jnp.where(mine, start, 0.0), axis=1, keepdims=True)
    length = jnp.sum(jnp.where(mine, lengths, 0.0), axis=1, keepdims=True)
    within = jnp.bitwise_and(slot, MOST - 1).astype(f32)
    source = jnp.where(within < length, begin + within, -1.0)
    placing = (iota((count, rows), 1).astype(f32) == source).astype(bf16)
    out_ref[...] = jnp.dot(placing, x_ref[...], preferred_element_type=f32).astype(bf16)


def place(sizes, meta, x_part, count):
    part = x_part.shape[1]
    vmem = pl.BlockSpec(memory_space=pltpu.VMEM)
    return pl.pallas_call(
        functools.partial(place_kernel, PLANE, sizes),
        out_shape=(
            jax.ShapeDtypeStruct((count, part), bf16),
            jax.ShapeDtypeStruct((8, 128), i32),
        ),
        in_specs=[vmem, vmem],
        out_specs=(vmem, vmem),
        compiler_params=params(),
    )(meta, x_part)


def unplace_kernel(plane, sizes, meta_ref, token_ref, out_ref):
    rows, count = out_ref.shape
    owner, start, lens = segment_rows(Meta(meta_ref, *sizes))
    row = iota((rows, 1), 0).astype(f32)
    inside = (row >= start) & (row < start + lens)
    target = jnp.sum(jnp.where(inside, owner * MOST + row - start, 0.0), axis=1, keepdims=True)
    slot = iota((1, count), 1)
    meant = slot_owner(slot, plane) * MOST + jnp.bitwise_and(slot, MOST - 1)
    out_ref[...] = (meant.astype(f32) == target).astype(bf16)


def choose_kernel(plane, sizes, meta_ref, token_ref, out_ref):
    meta = Meta(meta_ref, *sizes)
    count = out_ref.shape[0]
    rows = lax.axis_index("rows")
    z, at = lax.div(rows, plane), lax.rem(rows, plane)
    listed = meta_ref[pl.ds(pl.multiple_of(z * plane, plane), plane), : meta.slots]
    table = meta.table()
    ids = iota((1, meta.adapters), 1)
    lane = iota((plane, 128), 1)
    uses = jnp.zeros((plane, 128), f32)
    for q in range(8):
        step = (0, 4, 1, 7, 2, 6, 3, 5)[q]
        owner = jnp.bitwise_and(z + step, 7) * plane + at
        second = jnp.max(jnp.where(table == 2 * owner + 1, ids, -1), axis=1, keepdims=True)
        hit = jnp.max((listed == second).astype(f32), axis=1, keepdims=True)
        uses = jnp.where(lane == q, hit, uses)
    row = iota((count, 1), 0)
    both = 2 * MOST
    q_of = lax.div(row, both * plane) * 2 + jnp.bitwise_and(jnp.right_shift(row, 3), 1)
    source = lax.rem(lax.div(row, both), plane)
    spread = (source == iota((count, plane), 1)).astype(f32)
    wide = jnp.dot(spread, uses, preferred_element_type=f32)
    mine = iota((count, 128), 1) == q_of
    out_ref[...] = jnp.broadcast_to(
        jnp.sum(jnp.where(mine, wide, 0.0), axis=1, keepdims=True), out_ref.shape
    )


def pair_rows(x_ref, pair):
    tile = 2 * MOST
    return jnp.concatenate(
        [x_ref[at : at + tile, :] for at in range(pair * tile, x_ref.shape[0], 8 * MOST)], axis=0
    )


def turn(low, second):
    turned = pltpu.roll(low, low.shape[1] // 2, 1)
    return jnp.where(second, turned, low), jnp.where(second, low, turned)


def early_kernel(choice_ref, x_ref, own_ref, d1, u1, d2, u2, d3, u3, out_ref, kept_ref, b_ref):
    part = x_ref.shape[1]
    many, both = out_ref.shape[0] // 2, out_ref.shape[1]
    odd = jnp.bitwise_and(iota((many, both), 0), MOST) > 0
    second = [choice_ref[i * many : (i + 1) * many, :] > 0.5 for i in range(4)]
    kept = pair_rows(x_ref, 0)
    kept_ref[...] = kept
    sides = [turn(jnp.dot(kept, own_ref[:part], preferred_element_type=f32), second[0])]
    for i, (even_map, odd_map) in enumerate(((d1, u1), (d2, u2), (d3, u3))):
        a = jnp.concatenate([even_map[:part], odd_map[:part]], axis=1)
        each = jnp.dot(pair_rows(x_ref, i + 1), a, preferred_element_type=f32)
        sides.append(turn(jnp.where(odd, each[:, both:], each[:, :both]), second[i + 1]))
    for i, ref in enumerate((own_ref, d1, u1, d2, u2, d3, u3)):
        b_ref[i] = ref[part:]
    left = iota((many, both), 1) < both // 2
    out_ref[:many] = jnp.where(left, sides[0][0], sides[2][1])
    out_ref[many:] = jnp.where(left, sides[1][0], sides[3][1])


def final_kernel(choice_ref, kept_ref, a_ref, b_ref, early_ref, out_ref):
    many, part = kept_ref.shape
    both = out_ref.shape[1]
    cut = a_ref.shape[0]
    low = jnp.dot(kept_ref[:, :cut], a_ref[...], preferred_element_type=f32)
    low = low + jnp.dot(kept_ref[:, cut:], b_ref[: part - cut], preferred_element_type=f32)
    low = turn(low, choice_ref[:many, :] > 0.5)[0]
    odd = jnp.bitwise_and(iota((many, both), 0), MOST) > 0
    mine = odd & (iota((many, both), 1) < both // 2)
    out_ref[:many] = jnp.where(mine, low, early_ref[:many])
    out_ref[many:] = early_ref[many:]


def delta_kernel(choice_ref, p0, p1, p2, p3, maps_ref, last, out_ref):
    count, width = out_ref.shape
    half, both = p0.shape
    rank = both // 2
    tile = 2 * MOST
    low = (p0[...] + p1[...]) + (p2[...] + p3[...])
    turned = pltpu.roll(low, rank, 1)
    lane = iota((half, both), 1) < rank
    twice = jnp.concatenate([jnp.where(lane, low, turned), jnp.where(lane, turned, low)], axis=0)
    keep = (iota((count, both), 1) >= rank) == (choice_ref[...] > 0.5)
    low = jnp.where(keep, twice, 0.0)
    odd = jnp.bitwise_and(iota((count, both), 0), MOST) > 0
    spread = jnp.concatenate(
        [jnp.where(odd, 0.0, low), jnp.where(odd, low, 0.0)], axis=1
    ).astype(bf16)
    many = count // 4
    tail = last[last.shape[0] - width :]
    for pair in range(4):
        maps = (maps_ref[0], tail) if pair == 0 else (maps_ref[2 * pair - 1], maps_ref[2 * pair])
        wide = [
            jnp.concatenate([b[at : at + both] for at in range(0, width, both)], axis=1)
            for b in maps
        ]
        got = jnp.dot(
            spread[pair * many : (pair + 1) * many],
            jnp.concatenate(wide, axis=0),
            preferred_element_type=f32,
        ).astype(bf16)
        for i in range(many // tile):
            at = i * 8 * MOST + pair * tile
            out_ref[at : at + tile, :] = got[i * tile : (i + 1) * tile]


def vmem_spec():
    return pl.BlockSpec(memory_space=pltpu.VMEM)


def halves_kernel(a_ref, b_ref, a_out, b_out):
    a_out[...] = a_ref[...]
    b_out[...] = b_ref[...]


def halves(a, b):
    shape = (a.shape[0] // 2, a.shape[1])
    return pl.pallas_call(
        halves_kernel,
        out_shape=(jax.ShapeDtypeStruct(shape, a.dtype),) * 2,
        grid=(1,),
        in_specs=[pl.BlockSpec(shape, lambda i: (0, 0)), pl.BlockSpec(shape, lambda i: (1, 0))],
        out_specs=(pl.BlockSpec(shape, lambda i: (0, 0)),) * 2,
        cost_estimate=FREE,
        compiler_params=params(),
    )(a, b)


def vmem_call(kernel, outs, *args):
    return pl.pallas_call(
        kernel,
        out_shape=tuple(jax.ShapeDtypeStruct(shape, dtype) for shape, dtype in outs),
        in_specs=[vmem_spec()] * len(args),
        out_specs=(vmem_spec(),) * len(outs),
        cost_estimate=FREE,
        compiler_params=params(),
    )(*args)


def attend_kernel(scale, q_ref, nk_ref, k_ref, v_ref, len_ref, *refs):
    ctx_ref, own_ref = refs[-2:]
    rows, cache, width = k_ref.shape
    kv_heads = width // HEAD
    group = q_ref.shape[1] // width
    many = 8 * group
    row = jnp.bitwise_and(iota((many, 128), 0), 7)
    lane = iota((many, 128), 1)
    upper = row >= 4
    place_ok = jnp.right_shift(lane, 5) == jnp.bitwise_and(row, 3)
    cell = jnp.bitwise_and(lane, cache - 1)
    lane8 = iota((8, 128), 1)
    for pair in range(rows // 16):
        q16 = q_ref[pl.ds(pair * 16, 16), :].astype(f32)
        nk16 = nk_ref[pl.ds(pair * 16, 16), :].astype(f32)
        for sub in range(2):
            base = pair * 16 + sub * 8
            q8 = q16[sub * 8 : sub * 8 + 8]
            nk8 = nk16[sub * 8 : sub * 8 + 8]
            keys = k_ref[pl.ds(base, 8)].reshape(8 * cache, width)
            values = v_ref[pl.ds(base, 8)].reshape(8 * cache, width)
            lens = jnp.concatenate([len_ref[pl.ds(base, 8), :]] * group, axis=0)
            valid = place_ok & (cell < lens)
            own_tile = jnp.zeros((8, 128), f32)
            for h in range(kv_heads):
                cut = slice(h * HEAD, (h + 1) * HEAD)
                q = jnp.concatenate(
                    [q8[:, (h * group + g) * HEAD : (h * group + g + 1) * HEAD] for g in range(group)],
                    axis=0,
                )
                score = lax.dot_general(
                    q.astype(bf16), keys[:, cut], NT, preferred_element_type=f32
                )
                score = jnp.where(upper, score[:, 128:], score[:, :128]) * scale
                score = jnp.where(valid, score, -1e30)
                own = jnp.sum(
                    q * jnp.concatenate([nk8[:, cut]] * group, axis=0), axis=1, keepdims=True
                ) * scale
                top = jnp.maximum(jnp.max(score, axis=1, keepdims=True), own)
                weight = jnp.where(valid, jnp.exp(score - top), 0.0)
                e_own = jnp.exp(own - top)
                inv = 1.0 / (jnp.sum(weight, axis=1, keepdims=True) + e_own)
                split = jnp.concatenate(
                    [jnp.where(upper, 0.0, weight), jnp.where(upper, weight, 0.0)], axis=1
                ).astype(bf16)
                ctx = jnp.dot(split, values[:, cut], preferred_element_type=f32) * inv
                w_own = e_own.astype(bf16).astype(f32) * inv
                for g in range(group):
                    head = h * group + g
                    ctx_ref[pl.ds(base, 8), head * HEAD : (head + 1) * HEAD] = ctx[g * 8 : g * 8 + 8]
                    own_tile = jnp.where(lane8 == head, w_own[g * 8 : g * 8 + 8], own_tile)
            own_ref[pl.ds(base, 8), :] = own_tile


def attend(first, steps, queries, new_key, cache_keys, cache_values, lengths, before=()):
    rows, wide = queries.shape
    cache, width = cache_keys.shape[1:]
    step = 32
    return pl.pallas_call(
        functools.partial(attend_kernel, 1.0 / math.sqrt(HEAD)),
        out_shape=(
            jax.ShapeDtypeStruct((rows, wide), f32),
            jax.ShapeDtypeStruct((rows, 128), f32),
        ),
        grid=(steps,),
        in_specs=[
            pl.BlockSpec((step, wide), lambda i: (i + first, 0)),
            pl.BlockSpec((step, width), lambda i: (i + first, 0)),
            pl.BlockSpec((step, cache, width), lambda i: (i + first, 0, 0)),
            pl.BlockSpec((step, cache, width), lambda i: (i + first, 0, 0)),
            pl.BlockSpec((step, 1), lambda i: (i + first, 0)),
        ]
        + [pl.BlockSpec(memory_space=pl.ANY)] * len(before),
        out_specs=(
            pl.BlockSpec((step, wide), lambda i: (i + first, 0)),
            pl.BlockSpec((step, 128), lambda i: (i + first, 0)),
        ),
        input_output_aliases={5 + i: i for i in range(len(before))},
        cost_estimate=FREE,
        compiler_params=params(60),
    )(queries, new_key, cache_keys, cache_values, lengths, *before)


def finish_kernel(un_ref, delta_ref, base_ref, ctx_ref, own_ref, value_ref, out_ref):
    heads = out_ref.shape[1] // HEAD
    group = out_ref.shape[1] // value_ref.shape[1]
    delta = jnp.dot(un_ref[...], delta_ref[...], preferred_element_type=f32)
    value = (base_ref[...] + delta).astype(bf16)
    value_ref[...] = value
    value = value.astype(f32)
    for head in range(heads):
        kv = head // group
        cut = slice(head * HEAD, (head + 1) * HEAD)
        out_ref[:, cut] = (
            ctx_ref[:, cut] + own_ref[:, head : head + 1] * value[:, kv * HEAD : (kv + 1) * HEAD]
        ).astype(bf16)


def finish(un, delta, base, ctx, own):
    rows, wide = ctx.shape
    step = 128
    by_row = lambda n: pl.BlockSpec((step, n), lambda i: (i, 0))
    whole = lambda a: pl.BlockSpec(a.shape, lambda i: (0, 0))
    return pl.pallas_call(
        finish_kernel,
        out_shape=(
            jax.ShapeDtypeStruct(base.shape, bf16),
            jax.ShapeDtypeStruct((rows, wide), bf16),
        ),
        grid=(rows // step,),
        in_specs=[
            by_row(un.shape[1]),
            whole(delta),
            by_row(base.shape[1]),
            by_row(wide),
            by_row(128),
        ],
        out_specs=(by_row(base.shape[1]), by_row(wide)),
        compiler_params=params(),
    )(un, delta, base, ctx, own)


def body(
    normed_rows,
    value_weight,
    adapter_a,
    adapter_b,
    page_table,
    group_list,
    seg_len,
    kv_len,
    queries,
    new_key,
    cache_keys,
    cache_values,
):
    tp = lax.axis_size("tp")
    groups = lax.axis_size("rows")
    planes = groups // PLANE
    rows = normed_rows.shape[0]
    part = normed_rows.shape[1] // tp
    per_owner, _, rank = adapter_a.shape
    width = adapter_b.shape[2]
    count = groups * MOST
    slots, adapters = group_list.shape[1], page_table.shape[0]
    sizes = (groups, slots, adapters)
    wide = lambda x: jnp.pad(x, ((0, 0), (0, 128 - x.shape[1])))
    meta = jnp.concatenate([wide(group_list), wide(page_table.reshape(1, -1)), wide(seg_len)], axis=0)
    planes_of = [[z * PLANE + at for at in range(PLANE)] for z in range(planes)]
    both = per_owner * rank
    lengths = kv_len.reshape(-1, 1)

    def shift_z(x, by):
        return lax.ppermute(
            x, "rows", [(r, (r + by * PLANE) % groups) for r in range(groups)]
        )

    def over_plane(x):
        size, wide = x.shape
        x = lax.all_to_all(
            x.reshape(PLANE, size // PLANE, wide),
            "rows",
            split_axis=0,
            concat_axis=0,
            axis_index_groups=planes_of,
            tiled=True,
        )
        return x.reshape(size, wide)

    packed = jnp.concatenate(
        [jnp.swapaxes(adapter_a, 0, 1).reshape(part, both)]
        + [adapter_b.reshape(both, width)[:, at : at + both] for at in range(0, width, both)],
        axis=0,
    )
    up, down = [shift_z(packed, 1)], [shift_z(packed, -1)]

    packed, normed_rows, meta = lax.optimization_barrier((packed, normed_rows, meta))
    x_part = lax.dynamic_slice_in_dim(normed_rows, lax.axis_index("tp") * part, part, 1)
    placed, token = place(sizes, meta, x_part, count)
    arrived = over_plane(placed)
    (choice,) = vmem_call(
        functools.partial(choose_kernel, PLANE, sizes), [((count, both), f32)], meta, token
    )
    up[0], down[0], choice, queries, lengths = lax.optimization_barrier(
        (up[0], down[0], choice, queries, lengths)
    )
    up.append(shift_z(up[0], 1))
    down.append(shift_z(down[0], -1))
    steps = rows // 64
    done = attend(0, steps, queries, new_key, cache_keys, cache_values, lengths)
    up[1], down[1], done, queries = lax.optimization_barrier((up[1], down[1], done, queries))
    up.append(shift_z(up[1], 1))
    down.append(shift_z(down[1], -1))
    ctx, own = attend(steps, steps, queries, new_key, cache_keys, cache_values, lengths, done)
    up[2], down[2], ctx, own, meta = lax.optimization_barrier((up[2], down[2], ctx, own, meta))
    half_up, half_down = halves(up[2], down[2])
    last_a, last_b = shift_z(half_up, 1), shift_z(half_down, -1)
    (un,) = vmem_call(
        functools.partial(unplace_kernel, PLANE, sizes), [((rows, count), bf16)], meta, token
    )
    maps = [m for pair in zip(down, up) for m in pair]
    early, kept, b_maps = vmem_call(
        early_kernel,
        [((count // 2, both), f32), ((count // 4, part), bf16), ((7, width, both), bf16)],
        choice,
        arrived,
        packed,
        *maps,
    )
    last_a, last_b, early, kept, b_maps, un = lax.optimization_barrier(
        (last_a, last_b, early, kept, b_maps, un)
    )
    (partial,) = vmem_call(
        final_kernel, [((count // 2, both), f32)], choice, kept, last_a, last_b, early
    )
    others = [
        lax.ppermute(partial, "tp", [(j, (j + k) % tp) for j in range(tp)]) for k in range(1, tp)
    ]
    partial, normed_rows = lax.optimization_barrier((partial, normed_rows))
    base = jnp.dot(normed_rows, value_weight, preferred_element_type=f32)
    *others, base = lax.optimization_barrier((*others, base))
    (out,) = vmem_call(
        delta_kernel, [((count, width), bf16)], choice, partial, *others, b_maps, last_b
    )
    return finish(un, over_plane(out), base, ctx, own)


def solution(mesh):
    return jax.shard_map(
        body,
        mesh=mesh,
        in_specs=(
            P("rows", None),
            P(None, "tp"),
            P("rows", "tp", None),
            P("rows", None, "tp"),
            P(),
            P(),
            P("rows", None),
            P("rows", None),
            P("rows", "tp"),
            P("rows", "tp"),
            P("rows", None, "tp"),
            P("rows", None, "tp"),
        ),
        out_specs=(P("rows", "tp"), P("rows", "tp")),
        check_vma=False,
    )
```

```python
import functools
import math

import jax
import jax.numpy as jnp
from jax import lax
from jax.experimental import pallas as pl
from jax.experimental.pallas import tpu as pltpu
from jax.sharding import PartitionSpec as P

HEAD = 128
PLANE = 8
MOST = 8
f32 = jnp.float32
bf16 = jnp.bfloat16
i32 = jnp.int32
NT = (((1,), (1,)), ((), ()))
MIB = 1024 * 1024


FREE = pl.CostEstimate(flops=0, bytes_accessed=0, transcendentals=0)


def params(mib=12):
    return pltpu.CompilerParams(vmem_limit_bytes=mib * MIB)


def iota(shape, dim):
    return lax.broadcasted_iota(i32, shape, dim)


def segment_rows(meta):
    slots, groups = meta.slots, meta.groups
    adapters = meta.adapters
    listed = meta.ref[pl.ds(lax.axis_index("rows"), 1), :slots]
    hit = (iota((adapters, slots), 0) == listed).astype(f32)
    table = jnp.broadcast_to(meta.table().astype(f32), (8, adapters))
    position = jnp.dot(table, hit, preferred_element_type=f32)[:1]
    owner = jnp.right_shift(position.astype(i32), 1).astype(f32)
    lens = meta.ref[groups + 1 : groups + 2, :slots].astype(f32)
    before = (iota((slots, slots), 0) < iota((slots, slots), 1)).astype(f32)
    start = jnp.dot(jnp.broadcast_to(lens, (8, slots)), before, preferred_element_type=f32)[:1]
    return owner, start, lens


class Meta:
    def __init__(self, ref, groups, slots, adapters):
        self.ref, self.groups, self.slots, self.adapters = ref, groups, slots, adapters

    def table(self):
        return self.ref[self.groups : self.groups + 1, : self.adapters]


def ahead(q):
    i = jnp.right_shift(q, 1)
    odd = jnp.bitwise_and(q, 1) == 1
    return jnp.where(odd, jnp.where(i == 0, 4, 8 - i), i)


def slot_owner(slot, plane):
    z = lax.div(lax.axis_index("rows"), plane)
    q = jnp.bitwise_and(jnp.right_shift(slot, 3), 7)
    return jnp.bitwise_and(z + ahead(q), 7) * plane + jnp.right_shift(slot, 6)


def place_kernel(plane, sizes, meta_ref, x_ref, out_ref, token_ref):
    count = out_ref.shape[0]
    rows = x_ref.shape[0]
    token_ref[...] = jnp.zeros_like(token_ref)
    owner, start, lengths = segment_rows(Meta(meta_ref, *sizes))
    slot = iota((count, 1), 0)
    mine = owner == slot_owner(slot, plane).astype(f32)
    begin = jnp.sum(jnp.where(mine, start, 0.0), axis=1, keepdims=True)
    length = jnp.sum(jnp.where(mine, lengths, 0.0), axis=1, keepdims=True)
    within = jnp.bitwise_and(slot, MOST - 1).astype(f32)
    source = jnp.where(within < length, begin + within, -1.0)
    placing = (iota((count, rows), 1).astype(f32) == source).astype(bf16)
    out_ref[...] = jnp.dot(placing, x_ref[...], preferred_element_type=f32).astype(bf16)


def place(sizes, meta, x_part, count):
    part = x_part.shape[1]
    vmem = pl.BlockSpec(memory_space=pltpu.VMEM)
    return pl.pallas_call(
        functools.partial(place_kernel, PLANE, sizes),
        out_shape=(
            jax.ShapeDtypeStruct((count, part), bf16),
            jax.ShapeDtypeStruct((8, 128), i32),
        ),
        in_specs=[vmem, vmem],
        out_specs=(vmem, vmem),
        compiler_params=params(),
    )(meta, x_part)


def unplace_kernel(plane, sizes, meta_ref, token_ref, out_ref):
    rows, count = out_ref.shape
    owner, start, lens = segment_rows(Meta(meta_ref, *sizes))
    row = iota((rows, 1), 0).astype(f32)
    inside = (row >= start) & (row < start + lens)
    target = jnp.sum(jnp.where(inside, owner * MOST + row - start, 0.0), axis=1, keepdims=True)
    slot = iota((1, count), 1)
    meant = slot_owner(slot, plane) * MOST + jnp.bitwise_and(slot, MOST - 1)
    out_ref[...] = (meant.astype(f32) == target).astype(bf16)


def choose_kernel(plane, sizes, meta_ref, token_ref, out_ref):
    meta = Meta(meta_ref, *sizes)
    count = out_ref.shape[0]
    rows = lax.axis_index("rows")
    z, at = lax.div(rows, plane), lax.rem(rows, plane)
    listed = meta_ref[pl.ds(pl.multiple_of(z * plane, plane), plane), : meta.slots]
    table = meta.table()
    ids = iota((1, meta.adapters), 1)
    lane = iota((plane, 128), 1)
    uses = jnp.zeros((plane, 128), f32)
    for q in range(8):
        step = (0, 4, 1, 7, 2, 6, 3, 5)[q]
        owner = jnp.bitwise_and(z + step, 7) * plane + at
        second = jnp.max(jnp.where(table == 2 * owner + 1, ids, -1), axis=1, keepdims=True)
        hit = jnp.max((listed == second).astype(f32), axis=1, keepdims=True)
        uses = jnp.where(lane == q, hit, uses)
    row = iota((count, 1), 0)
    both = 2 * MOST
    q_of = lax.div(row, both * plane) * 2 + jnp.bitwise_and(jnp.right_shift(row, 3), 1)
    source = lax.rem(lax.div(row, both), plane)
    spread = (source == iota((count, plane), 1)).astype(f32)
    wide = jnp.dot(spread, uses, preferred_element_type=f32)
    mine = iota((count, 128), 1) == q_of
    out_ref[...] = jnp.broadcast_to(
        jnp.sum(jnp.where(mine, wide, 0.0), axis=1, keepdims=True), out_ref.shape
    )


def pair_rows(x_ref, pair):
    tile = 2 * MOST
    return jnp.concatenate(
        [x_ref[at : at + tile, :] for at in range(pair * tile, x_ref.shape[0], 8 * MOST)], axis=0
    )


def turn(low, second):
    turned = pltpu.roll(low, low.shape[1] // 2, 1)
    return jnp.where(second, turned, low), jnp.where(second, low, turned)


def early_kernel(choice_ref, x_ref, own_ref, d1, u1, d2, u2, d3, u3, out_ref, kept_ref):
    part = x_ref.shape[1]
    many, both = out_ref.shape[0] // 2, out_ref.shape[1]
    odd = jnp.bitwise_and(iota((many, both), 0), MOST) > 0
    second = [choice_ref[i * many : (i + 1) * many, :] > 0.5 for i in range(4)]
    kept = pair_rows(x_ref, 0)
    kept_ref[...] = kept
    sides = [turn(jnp.dot(kept, own_ref[:part], preferred_element_type=f32), second[0])]
    for i, (even_map, odd_map) in enumerate(((d1, u1), (d2, u2), (d3, u3))):
        a = jnp.concatenate([even_map[:part], odd_map[:part]], axis=1)
        each = jnp.dot(pair_rows(x_ref, i + 1), a, preferred_element_type=f32)
        sides.append(turn(jnp.where(odd, each[:, both:], each[:, :both]), second[i + 1]))
    left = iota((many, both), 1) < both // 2
    out_ref[:many] = jnp.where(left, sides[0][0], sides[2][1])
    out_ref[many:] = jnp.where(left, sides[1][0], sides[3][1])


def final_kernel(choice_ref, kept_ref, a_ref, b_ref, early_ref, out_ref):
    many, part = kept_ref.shape
    both = out_ref.shape[1]
    cut = a_ref.shape[0]
    low = jnp.dot(kept_ref[:, :cut], a_ref[...], preferred_element_type=f32)
    low = low + jnp.dot(kept_ref[:, cut:], b_ref[: part - cut], preferred_element_type=f32)
    low = turn(low, choice_ref[:many, :] > 0.5)[0]
    odd = jnp.bitwise_and(iota((many, both), 0), MOST) > 0
    mine = odd & (iota((many, both), 1) < both // 2)
    out_ref[:many] = jnp.where(mine, low, early_ref[:many]).astype(bf16)
    out_ref[many:] = early_ref[many:].astype(bf16)


def delta_kernel(choice_ref, p0, p1, p2, p3, own, last, d1, u1, d2, u2, d3, u3, out_ref):
    count, width = out_ref.shape
    half, both = p0.shape
    rank = both // 2
    tile = 2 * MOST
    own_low, *rest = [p[...].astype(f32) for p in (p0, p1, p2, p3)]
    low = (own_low + rest[0]) + (rest[1] + rest[2])
    turned = pltpu.roll(low, rank, 1)
    lane = iota((half, both), 1) < rank
    twice = jnp.concatenate([jnp.where(lane, low, turned), jnp.where(lane, turned, low)], axis=0)
    keep = (iota((count, both), 1) >= rank) == (choice_ref[...] > 0.5)
    low = jnp.where(keep, twice, 0.0)
    odd = jnp.bitwise_and(iota((count, both), 0), MOST) > 0
    spread = jnp.concatenate(
        [jnp.where(odd, 0.0, low), jnp.where(odd, low, 0.0)], axis=1
    ).astype(bf16)
    many = count // 4
    for pair, refs in enumerate(((own, last), (d1, u1), (d2, u2), (d3, u3))):
        wide = []
        for ref in refs:
            first = ref.shape[0] - width
            wide.append(
                jnp.concatenate(
                    [ref[first + at : first + at + both] for at in range(0, width, both)], axis=1
                )
            )
        got = jnp.dot(
            spread[pair * many : (pair + 1) * many],
            jnp.concatenate(wide, axis=0),
            preferred_element_type=f32,
        ).astype(bf16)
        for i in range(many // tile):
            at = i * 8 * MOST + pair * tile
            out_ref[at : at + tile, :] = got[i * tile : (i + 1) * tile]


def vmem_spec():
    return pl.BlockSpec(memory_space=pltpu.VMEM)


def halves_kernel(a_ref, b_ref, a_out, b_out):
    a_out[...] = a_ref[...]
    b_out[...] = b_ref[...]


def halves(a, b):
    shape = (a.shape[0] // 2, a.shape[1])
    return pl.pallas_call(
        halves_kernel,
        out_shape=(jax.ShapeDtypeStruct(shape, a.dtype),) * 2,
        grid=(1,),
        in_specs=[pl.BlockSpec(shape, lambda i: (0, 0)), pl.BlockSpec(shape, lambda i: (1, 0))],
        out_specs=(pl.BlockSpec(shape, lambda i: (0, 0)),) * 2,
        cost_estimate=FREE,
        compiler_params=params(),
    )(a, b)


def delta_call(choice, parts, maps, count, width):
    def whole(a):
        return pl.BlockSpec(a.shape, lambda i: (0, 0))

    def tail(a):
        last = a.shape[0] // width - 1
        return pl.BlockSpec((width, a.shape[1]), lambda i: (last, 0))

    return pl.pallas_call(
        delta_kernel,
        out_shape=jax.ShapeDtypeStruct((count, width), bf16),
        grid=(1,),
        in_specs=[whole(a) for a in (choice, *parts)]
        + [tail(a) if a.shape[0] % width == 0 else whole(a) for a in maps],
        out_specs=pl.BlockSpec((count, width), lambda i: (0, 0)),
        compiler_params=params(),
    )(choice, *parts, *maps)


def vmem_call(kernel, outs, *args):
    return pl.pallas_call(
        kernel,
        out_shape=tuple(jax.ShapeDtypeStruct(shape, dtype) for shape, dtype in outs),
        in_specs=[vmem_spec()] * len(args),
        out_specs=(vmem_spec(),) * len(outs),
        cost_estimate=FREE,
        compiler_params=params(),
    )(*args)


def attend_kernel(scale, q_ref, nk_ref, k_ref, v_ref, len_ref, *refs):
    ctx_ref, own_ref = refs[-2:]
    rows, cache, width = k_ref.shape
    kv_heads = width // HEAD
    group = q_ref.shape[1] // width
    many = 8 * group
    row = jnp.bitwise_and(iota((many, 128), 0), 7)
    lane = iota((many, 128), 1)
    upper = row >= 4
    place_ok = jnp.right_shift(lane, 5) == jnp.bitwise_and(row, 3)
    cell = jnp.bitwise_and(lane, cache - 1)
    lane8 = iota((8, 128), 1)
    for pair in range(rows // 16):
        q16 = q_ref[pl.ds(pair * 16, 16), :].astype(f32)
        nk16 = nk_ref[pl.ds(pair * 16, 16), :].astype(f32)
        for sub in range(2):
            base = pair * 16 + sub * 8
            q8 = q16[sub * 8 : sub * 8 + 8]
            nk8 = nk16[sub * 8 : sub * 8 + 8]
            keys = k_ref[pl.ds(base, 8)].reshape(8 * cache, width)
            values = v_ref[pl.ds(base, 8)].reshape(8 * cache, width)
            lens = jnp.concatenate([len_ref[pl.ds(base, 8), :]] * group, axis=0)
            valid = place_ok & (cell < lens)
            own_tile = jnp.zeros((8, 128), f32)
            for h in range(kv_heads):
                cut = slice(h * HEAD, (h + 1) * HEAD)
                q = jnp.concatenate(
                    [q8[:, (h * group + g) * HEAD : (h * group + g + 1) * HEAD] for g in range(group)],
                    axis=0,
                )
                score = lax.dot_general(
                    q.astype(bf16), keys[:, cut], NT, preferred_element_type=f32
                )
                score = jnp.where(upper, score[:, 128:], score[:, :128]) * scale
                score = jnp.where(valid, score, -1e30)
                own = jnp.sum(
                    q * jnp.concatenate([nk8[:, cut]] * group, axis=0), axis=1, keepdims=True
                ) * scale
                top = jnp.maximum(jnp.max(score, axis=1, keepdims=True), own)
                weight = jnp.where(valid, jnp.exp(score - top), 0.0)
                e_own = jnp.exp(own - top)
                inv = 1.0 / (jnp.sum(weight, axis=1, keepdims=True) + e_own)
                split = jnp.concatenate(
                    [jnp.where(upper, 0.0, weight), jnp.where(upper, weight, 0.0)], axis=1
                ).astype(bf16)
                ctx = jnp.dot(split, values[:, cut], preferred_element_type=f32) * inv
                w_own = e_own.astype(bf16).astype(f32) * inv
                for g in range(group):
                    head = h * group + g
                    ctx_ref[pl.ds(base, 8), head * HEAD : (head + 1) * HEAD] = ctx[g * 8 : g * 8 + 8]
                    own_tile = jnp.where(lane8 == head, w_own[g * 8 : g * 8 + 8], own_tile)
            own_ref[pl.ds(base, 8), :] = own_tile


def attend(first, steps, queries, new_key, cache_keys, cache_values, lengths, before=()):
    rows, wide = queries.shape
    cache, width = cache_keys.shape[1:]
    step = 32
    return pl.pallas_call(
        functools.partial(attend_kernel, 1.0 / math.sqrt(HEAD)),
        out_shape=(
            jax.ShapeDtypeStruct((rows, wide), f32),
            jax.ShapeDtypeStruct((rows, 128), f32),
        ),
        grid=(steps,),
        in_specs=[
            pl.BlockSpec((step, wide), lambda i: (i + first, 0)),
            pl.BlockSpec((step, width), lambda i: (i + first, 0)),
            pl.BlockSpec((step, cache, width), lambda i: (i + first, 0, 0)),
            pl.BlockSpec((step, cache, width), lambda i: (i + first, 0, 0)),
            pl.BlockSpec((step, 1), lambda i: (i + first, 0)),
        ]
        + [pl.BlockSpec(memory_space=pl.ANY)] * len(before),
        out_specs=(
            pl.BlockSpec((step, wide), lambda i: (i + first, 0)),
            pl.BlockSpec((step, 128), lambda i: (i + first, 0)),
        ),
        input_output_aliases={5 + i: i for i in range(len(before))},
        cost_estimate=FREE,
        compiler_params=params(60),
    )(queries, new_key, cache_keys, cache_values, lengths, *before)


def finish_kernel(un_ref, delta_ref, base_ref, ctx_ref, own_ref, value_ref, out_ref):
    heads = out_ref.shape[1] // HEAD
    group = out_ref.shape[1] // value_ref.shape[1]
    delta = jnp.dot(un_ref[...], delta_ref[...], preferred_element_type=f32)
    value = (base_ref[...] + delta).astype(bf16)
    value_ref[...] = value
    value = value.astype(f32)
    for head in range(heads):
        kv = head // group
        cut = slice(head * HEAD, (head + 1) * HEAD)
        out_ref[:, cut] = (
            ctx_ref[:, cut] + own_ref[:, head : head + 1] * value[:, kv * HEAD : (kv + 1) * HEAD]
        ).astype(bf16)


def finish(un, delta, base, ctx, own):
    rows, wide = ctx.shape
    step = 128
    by_row = lambda n: pl.BlockSpec((step, n), lambda i: (i, 0))
    whole = lambda a: pl.BlockSpec(a.shape, lambda i: (0, 0))
    return pl.pallas_call(
        finish_kernel,
        out_shape=(
            jax.ShapeDtypeStruct(base.shape, bf16),
            jax.ShapeDtypeStruct((rows, wide), bf16),
        ),
        grid=(rows // step,),
        in_specs=[
            by_row(un.shape[1]),
            whole(delta),
            by_row(base.shape[1]),
            by_row(wide),
            by_row(128),
        ],
        out_specs=(by_row(base.shape[1]), by_row(wide)),
        compiler_params=params(),
    )(un, delta, base, ctx, own)


def body(
    normed_rows,
    value_weight,
    adapter_a,
    adapter_b,
    page_table,
    group_list,
    seg_len,
    kv_len,
    queries,
    new_key,
    cache_keys,
    cache_values,
):
    tp = lax.axis_size("tp")
    groups = lax.axis_size("rows")
    planes = groups // PLANE
    rows = normed_rows.shape[0]
    part = normed_rows.shape[1] // tp
    per_owner, _, rank = adapter_a.shape
    width = adapter_b.shape[2]
    count = groups * MOST
    slots, adapters = group_list.shape[1], page_table.shape[0]
    sizes = (groups, slots, adapters)
    wide = lambda x: jnp.pad(x, ((0, 0), (0, 128 - x.shape[1])))
    meta = jnp.concatenate([wide(group_list), wide(page_table.reshape(1, -1)), wide(seg_len)], axis=0)
    planes_of = [[z * PLANE + at for at in range(PLANE)] for z in range(planes)]
    both = per_owner * rank
    lengths = kv_len.reshape(-1, 1)

    def shift_z(x, by):
        return lax.ppermute(
            x, "rows", [(r, (r + by * PLANE) % groups) for r in range(groups)]
        )

    def over_plane(x):
        size, wide = x.shape
        x = lax.all_to_all(
            x.reshape(PLANE, size // PLANE, wide),
            "rows",
            split_axis=0,
            concat_axis=0,
            axis_index_groups=planes_of,
            tiled=True,
        )
        return x.reshape(size, wide)

    packed = jnp.concatenate(
        [jnp.swapaxes(adapter_a, 0, 1).reshape(part, both)]
        + [adapter_b.reshape(both, width)[:, at : at + both] for at in range(0, width, both)],
        axis=0,
    )
    up, down = [shift_z(packed, 1)], [shift_z(packed, -1)]

    packed, normed_rows, meta = lax.optimization_barrier((packed, normed_rows, meta))
    x_part = lax.dynamic_slice_in_dim(normed_rows, lax.axis_index("tp") * part, part, 1)
    placed, token = place(sizes, meta, x_part, count)
    arrived = over_plane(placed)
    (choice,) = vmem_call(
        functools.partial(choose_kernel, PLANE, sizes), [((count, both), f32)], meta, token
    )
    up[0], down[0], choice, queries, lengths = lax.optimization_barrier(
        (up[0], down[0], choice, queries, lengths)
    )
    up.append(shift_z(up[0], 1))
    down.append(shift_z(down[0], -1))
    steps = rows // 64
    done = attend(0, steps, queries, new_key, cache_keys, cache_values, lengths)
    up[1], down[1], done, queries = lax.optimization_barrier((up[1], down[1], done, queries))
    up.append(shift_z(up[1], 1))
    down.append(shift_z(down[1], -1))
    ctx, own = attend(steps, steps, queries, new_key, cache_keys, cache_values, lengths, done)
    up[2], down[2], ctx, own, meta = lax.optimization_barrier((up[2], down[2], ctx, own, meta))
    half_up, half_down = halves(up[2], down[2])
    last_a, last_b = shift_z(half_up, 1), shift_z(half_down, -1)
    (un,) = vmem_call(
        functools.partial(unplace_kernel, PLANE, sizes), [((rows, count), bf16)], meta, token
    )
    maps = [m for pair in zip(down, up) for m in pair]
    early, kept = vmem_call(
        early_kernel,
        [((count // 2, both), f32), ((count // 4, part), bf16)],
        choice,
        arrived,
        packed,
        *maps,
    )
    last_a, last_b, early, kept, un = lax.optimization_barrier((last_a, last_b, early, kept, un))
    (partial,) = vmem_call(
        final_kernel, [((count // 2, both), bf16)], choice, kept, last_a, last_b, early
    )
    others = [
        lax.ppermute(partial, "tp", [(j, (j + k) % tp) for j in range(tp)]) for k in range(1, tp)
    ]
    partial, normed_rows = lax.optimization_barrier((partial, normed_rows))
    base = jnp.dot(normed_rows, value_weight, preferred_element_type=f32)
    *others, base = lax.optimization_barrier((*others, base))
    out = delta_call(choice, [partial, *others], [packed, last_b, *maps], count, width)
    return finish(un, over_plane(out), base, ctx, own)


def solution(mesh):
    return jax.shard_map(
        body,
        mesh=mesh,
        in_specs=(
            P("rows", None),
            P(None, "tp"),
            P("rows", "tp", None),
            P("rows", None, "tp"),
            P(),
            P(),
            P("rows", None),
            P("rows", None),
            P("rows", "tp"),
            P("rows", "tp"),
            P("rows", None, "tp"),
            P("rows", None, "tp"),
        ),
        out_specs=(P("rows", "tp"), P("rows", "tp")),
        check_vma=False,
    )
```
